256 devices in a mesh: section: 4 (over y_hi, core), expert: 64 (over z, x, y_lo).
Axes of the slice: x: 4, y: 4 (y_hi: 2, y_lo: 2; y = y_hi * 2 + y_lo), z: 8, core: 2. Of those that a mesh axis runs over, the one named last changes fastest.
Arguments:
- previous: bfloat16 [4, 64, 128, 1024], P('section', 'expert'), may hold values from -6 to 6
- encoder_states: bfloat16 [64, 1024, 1024], P('expert', 'section'), may hold values from -150 to 150
- routes: int32 [4, 64, 128, 2], P('section', 'expert'), may hold values from 0 to 31, all different within a row; in each aligned block of 128 rows (0 to 127, 128 to 255, ..., all dimensions but the last counted through in order) at most 12 rows name the same one
- gate_values: float32 [4, 64, 128, 2], P('section', 'expert'), may hold values from 0.1 to 1
- gain_attn: float32 [4, 1024], P('section'), may hold values from 0.25 to 1.75
- gain_moe: float32 [4, 1024], P('section'), may hold values from 0.25 to 1.75
- query_weight: bfloat16 [4, 1024, 1024], P('section', 'expert'), may hold values from -0.1875 to 0.1875
- key_weight: bfloat16 [4, 1024, 1024], P('section', 'expert'), may hold values from -0.1875 to 0.1875
- value_weight: bfloat16 [4, 1024, 1024], P('section', 'expert'), may hold values from -0.1875 to 0.1875
- out_weight: bfloat16 [4, 1024, 1024], P('section', 'expert'), may hold values from -0.1875 to 0.1875
- expert_gate: bfloat16 [4, 64, 1024, 1408], P('section', 'expert'), may hold values from -0.1875 to 0.1875
- expert_up: bfloat16 [4, 64, 1024, 1408], P('section', 'expert'), may hold values from -0.1875 to 0.1875
- expert_down: bfloat16 [4, 64, 1408, 1024], P('section', 'expert'), may hold values from -0.109375 to 0.109375
Outputs:
- following: bfloat16 [4, 64, 128, 1024], P('section', 'expert')
The draws below stay inside these ranges and needn't reach their ends.
Inputs may be any that keep to these rules, and one draw needn't show every extreme that they name: In the rows of one index of expert (each section apart) no expert is named by more than 12 routes; the two experts of a token differ.
All inputs are finite; a program needn't handle non-finite values.
Results may differ from the reference program's by a relative error of at most 0.015.
The reference program's roundings to bfloat16 on the way count: a program that leaves them out, or rounds other values in their place, can miss the bound.
Values may be sent and summed in bfloat16 or wider, within the bound.
A program may use at most 128 MiB of HBM per device.

```python
import math
import jax
import jax.numpy as jnp
import numpy as np
from jax import lax

D = 1024
HEADS = 16
FF = 2816
EXPERTS = 32
DEC = 128
ENC = 1024
TOK_DEV = 128
SEQS = 64
CAP = 12
SPLIT = 2
PIECE = 1408
N_SECTION = 4
N_EXPERT = 64


def draw_encoder_states(key, part):
    key = jax.random.fold_in(key, 7)
    first = jax.random.fold_in(key, 0)
    return jnp.clip(jax.random.normal(first, (SEQS, ENC, D)), -5.0, 5.0).astype(jnp.bfloat16)


def block_levels(own_key, shape, cuts, least, top_value):
    level, own = 1.0, jax.random.fold_in(own_key, 6)
    for position, parts in cuts:
        steps = jnp.exp(jax.random.uniform(jax.random.fold_in(own, position), (parts,), jnp.float32, least / len(cuts), top_value / len(cuts)))
        level = level * jnp.repeat(steps, shape[position] // parts).reshape([-1 if axis == position else 1 for axis in range(len(shape))])
    return level


def deal_out(stream_key, own, number, rows, number_of, top, bound, lean):
    ranking = jax.random.permutation(stream_key, number_of)
    packed, common = load_shares(number_of, rows * top, bound, lean, True), load_shares(number_of, rows * top, bound, lean, False)
    places = jnp.arange(number_of)

    def named(tallies, rotation):
        used = int((tallies > 0).sum())
        fixed = max(1, used // 4)
        passed = fixed + (places - fixed + rotation * (used - fixed)) % max(1, number_of - fixed)
        return jnp.zeros((number_of,), jnp.int32).at[ranking[jnp.where(places < fixed, places, passed)]].set(jnp.asarray(tallies, jnp.int32))

    tallies = jnp.where(number % 4 == 0, named(packed, number // 4), named(common, number - number // 4 - 1))
    mixed = jax.random.permutation(jax.random.fold_in(own, 3), number_of)
    donor, sink = mixed[0:number_of // 2 * 2:2], mixed[1:number_of // 2 * 2:2]
    room = jnp.minimum(tallies[donor] - 1, bound - tallies[sink]) // 2
    room = jnp.where((donor == ranking[0]) | (sink == ranking[0]) | (tallies[sink] == 0), 0, jnp.maximum(room, 0))
    passed = jax.random.randint(jax.random.fold_in(own, 4), (number_of // 2,), 0, 1 << 20) % (room + 1)
    tallies = tallies.at[donor].add(-passed).at[sink].add(passed)
    items = jnp.searchsorted(jnp.cumsum(tallies), jnp.arange(rows * top), side="right").astype(jnp.int32)
    listing = items.reshape(top, rows).T
    listing = listing[jax.random.permutation(jax.random.fold_in(own, 1), rows)]
    rotation = jax.random.randint(jax.random.fold_in(own, 2), (rows, 1), 0, top)
    return jnp.take_along_axis(listing, (jnp.arange(top)[None, :] + rotation) % top, axis=1)


def load_shares(number_of, total, most, slope, full):
    weights = [(1 << 20) // math.isqrt(grade ** slope) + 1 for grade in range(1, number_of + 1)]
    largest = most if full else min(most, max(-(-total // number_of), total * weights[0] // sum(weights)))
    least = 1 if total - largest >= number_of - 1 else 0
    holding, spare = [largest] + [least] * (number_of - 1), total - largest - least * (number_of - 1)
    while spare > 0:
        movable = [i for i in range(1, number_of) if holding[i] < largest] or [i for i in range(1, number_of) if holding[i] < most]
        whole, left = sum([weights[i] for i in movable]), spare
        for i in movable:
            addition = min(most - holding[i], max(1, left * weights[i] // whole), spare)
            holding[i] = holding[i] + addition
            spare = spare - addition
    return np.array(holding)


def centred(key, dims, deviation, reach, cuts=(), kind=jnp.bfloat16):
    array = jax.random.normal(key, dims, jnp.float32) * deviation
    if len(cuts) > 0:
        array = block_levels(key, dims, cuts, -0.22, 0.18) * array
    return jnp.clip(array, min=-reach, max=reach).astype(kind)


def setup_inputs(seed: int = 0) -> dict:
    arg_keys = jax.random.split(jax.random.key(seed), 14)
    previous = centred(arg_keys[0], (N_SECTION, SEQS, DEC, D), 1.0, 6.0, ((0, 4), (1, 64)))
    encoder_states = draw_encoder_states(jax.random.fold_in(arg_keys[13], 71), 0)
    routes_keys = jax.random.split(jax.random.fold_in(arg_keys[2], 1), N_SECTION * SEQS * DEC // TOK_DEV)
    routes_turns = jax.random.permutation(jax.random.fold_in(arg_keys[2], 3), N_SECTION * SEQS * DEC // TOK_DEV)
    routes = jax.vmap(lambda own, number: deal_out(jax.random.fold_in(arg_keys[2], 2), own, number, TOK_DEV, EXPERTS, 2, CAP, 2))(routes_keys, routes_turns).reshape((N_SECTION, SEQS, DEC, 2))
    gate_values = jnp.clip(0.1 + 0.9 * jax.random.uniform(arg_keys[3], (N_SECTION, SEQS, DEC, 2), jnp.float32) ** block_levels(arg_keys[3], (N_SECTION, SEQS, DEC, 2), ((0, 4), (1, 64)), -0.2, 0.2), 0.1, 1.0)
    gain_attn = jnp.clip(1.0 + 0.15 * jax.random.normal(arg_keys[4], (N_SECTION, D), jnp.float32), 0.25, 1.75)
    gain_moe = jnp.clip(1.0 + 0.15 * jax.random.normal(arg_keys[5], (N_SECTION, D), jnp.float32), 0.25, 1.75)
    query_weight = centred(arg_keys[6], (N_SECTION, D, D), D ** -0.5, 0.1875, ((0, 4), (1, 64)))
    key_weight = centred(arg_keys[7], (N_SECTION, D, D), D ** -0.5, 0.1875, ((0, 4), (1, 64)))
    value_weight = centred(arg_keys[8], (N_SECTION, D, D), D ** -0.5, 0.1875, ((0, 4), (1, 64)))
    out_weight = centred(arg_keys[9], (N_SECTION, D, D), D ** -0.5, 0.1875, ((0, 4), (1, 64)))
    expert_gate = centred(arg_keys[10], (N_SECTION, EXPERTS * SPLIT, D, PIECE), D ** -0.5, 0.1875, ((0, 4), (1, 64)))
    expert_up = centred(arg_keys[11], (N_SECTION, EXPERTS * SPLIT, D, PIECE), D ** -0.5, 0.1875, ((0, 4), (1, 64)))
    expert_down = centred(arg_keys[12], (N_SECTION, EXPERTS * SPLIT, PIECE, D), FF ** -0.5, 0.109375, ((0, 4), (1, 64)))
    return dict(previous=previous, encoder_states=encoder_states, routes=routes, gate_values=gate_values, gain_attn=gain_attn, gain_moe=gain_moe, query_weight=query_weight, key_weight=key_weight, value_weight=value_weight, out_weight=out_weight, expert_gate=expert_gate, expert_up=expert_up, expert_down=expert_down)


eps = 1e-06

def rms_scale(x, gain):
    return x * lax.rsqrt(lax.optimization_barrier(jnp.mean(x * x, axis=-1, keepdims=True)) + eps) * gain

def route_positions(flat):
    onehot = (flat[:, None] == jnp.arange(EXPERTS, dtype=jnp.int32)[None, :]).astype(jnp.int32)
    before = jnp.cumsum(onehot, axis=0) - onehot
    slot = lax.optimization_barrier(jnp.sum(before * onehot, axis=1))
    return (flat * CAP + slot).astype(jnp.int32)

def attend(item):
    query, keys, values = item
    head = query.shape[-1]
    scores = jnp.einsum('qhd,khd->hqk', query.astype(jnp.float32), keys.astype(jnp.float32)) * head ** (-0.5)
    top = lax.optimization_barrier(jnp.max(scores, axis=-1, keepdims=True))
    expo = jnp.exp(scores - top)
    probs = (expo / lax.optimization_barrier(jnp.sum(expo, axis=-1, keepdims=True))).astype(jnp.bfloat16)
    context = jnp.einsum('hqk,khd->qhd', probs.astype(jnp.float32), values.astype(jnp.float32))
    return context.astype(jnp.bfloat16)

def reference(previous, encoder_states, routes, gate_values, gain_attn, gain_moe, query_weight, key_weight, value_weight, out_weight, expert_gate, expert_up, expert_down):
    split = max(N_EXPERT // EXPERTS, 1)
    head = D // HEADS
    incoming = jnp.roll(previous, 1, axis=0)
    enc_rows = encoder_states.reshape(-1, D)
    results = []
    for section in range(N_SECTION):
        tokens = incoming[section].reshape(-1, D)
        normed = rms_scale(tokens.astype(jnp.float32), gain_attn[section]).astype(jnp.bfloat16)
        query = jnp.dot(normed, query_weight[section], preferred_element_type=jnp.float32).astype(jnp.bfloat16)
        keys = jnp.dot(enc_rows, key_weight[section], preferred_element_type=jnp.float32).astype(jnp.bfloat16)
        values = jnp.dot(enc_rows, value_weight[section], preferred_element_type=jnp.float32).astype(jnp.bfloat16)
        context = lax.map(attend, (query.reshape(SEQS, DEC, HEADS, head), keys.reshape(SEQS, ENC, HEADS, head), values.reshape(SEQS, ENC, HEADS, head)))
        attn_out = jnp.dot(context.reshape(-1, D), out_weight[section], preferred_element_type=jnp.float32)
        mixed = (tokens.astype(jnp.float32) + attn_out).astype(jnp.bfloat16)
        moe_in = rms_scale(mixed.astype(jnp.float32), gain_moe[section]).astype(jnp.bfloat16)
        flat = routes[section].reshape(N_EXPERT, 2 * TOK_DEV)
        positions = jax.vmap(route_positions)(flat)
        repeated = jnp.repeat(moe_in.reshape(N_EXPERT, TOK_DEV, D), 2, axis=1)
        device_ids = jnp.arange(N_EXPERT, dtype=jnp.int32)[:, None]
        buffer = jnp.zeros((N_EXPERT, EXPERTS * CAP, D), jnp.bfloat16).at[device_ids, positions].set(repeated)
        buffer = buffer.reshape(N_EXPERT, EXPERTS, CAP, D).transpose(1, 0, 2, 3).reshape(EXPERTS, N_EXPERT * CAP, D)

        def run_expert(item):
            rows, w_gate, w_up, w_down = item
            total = jnp.zeros((rows.shape[0], D), jnp.float32)
            for piece in range(split):
                gated = jnp.dot(rows, w_gate[piece], preferred_element_type=jnp.float32)
                upper = jnp.dot(rows, w_up[piece], preferred_element_type=jnp.float32)
                hidden = (jax.nn.gelu(gated) * upper).astype(jnp.bfloat16)
                total = total + jnp.dot(hidden, w_down[piece], preferred_element_type=jnp.float32)
            return total.astype(jnp.bfloat16)
        expert_out = lax.map(run_expert, (buffer, expert_gate[section].reshape(EXPERTS, split, D, PIECE), expert_up[section].reshape(EXPERTS, split, D, PIECE), expert_down[section].reshape(EXPERTS, split, PIECE, D)))
        flat_out = expert_out.reshape(EXPERTS, N_EXPERT, CAP, D).transpose(1, 0, 2, 3).reshape(N_EXPERT, EXPERTS * CAP, D)
        picked = flat_out[device_ids, positions]
        weights = gate_values[section].reshape(N_EXPERT, 2 * TOK_DEV)
        moe = (picked.astype(jnp.float32) * weights[:, :, None]).reshape(N_EXPERT, TOK_DEV, 2, D).sum(axis=2)
        result = (mixed.reshape(N_EXPERT, TOK_DEV, D).astype(jnp.float32) + moe).astype(jnp.bfloat16)
        results.append(result.reshape(SEQS, DEC, D))
    return jnp.stack(results, axis=0)
```

```python
import functools

import jax
import jax.numpy as jnp
import numpy as np
from jax import lax
from jax.experimental import pallas as pl
from jax.experimental.pallas import tpu as pltpu
from jax.sharding import PartitionSpec as P

EXPERTS = 32
CAP = 12
NZ, NX, NY = 8, 4, 4
DEC, ENC, D = 128, 1024, 1024
HALF = D // 2
QUART = D // 4
PIECE = 1408
SLOTS = EXPERTS * CAP
EPS = 1e-06
MESH = pl.DeviceIdType.MESH
BF, F32 = jnp.bfloat16, jnp.float32


def place_of():
    s, e = lax.axis_index("section"), lax.axis_index("expert")
    return e // 8, (e // 2) % NX, (s // 2) * 2 + e % 2, s % 2


def device(z, x, y, core):
    return ((y // 2) * 2 + core, (z * NX + x) * 2 + y % 2)


class Sems:
    def __init__(self, ref):
        self.ref, self.used = ref, 0

    def take(self, count=1):
        first = self.used
        self.used += count
        return first


def rms(x, gain):
    return x * lax.rsqrt(jnp.mean(x * x, axis=-1, keepdims=True) + EPS) * gain


def dot(a, b):
    return jnp.dot(a, b, preferred_element_type=F32)


SEMS_A = 160


def attention_kernel(prev, enc, wq, wk, wv, wo, gain, out, E, W, T, K, V, Q, C, MX, H, GM, ssem, rsem):
    z, x, y, b = place_of()
    a, yhi = y % 2, y // 2
    zp, zm = (z + 1) % NZ, (z + NZ - 1) % NZ
    xp, xm, xo = (x + 1) % NX, (x + NX - 1) % NX, (x + 2) % NX
    yp, ym, yo = (y + 1) % NY, (y + NY - 1) % NY, (y + 2) % NY
    mate = device(z, x, y, 1 - b)
    take = Sems(rsem).take
    pending = []

    bar = pltpu.get_barrier_semaphore()
    shift_src = (y + 3) % NY
    greet = [
        mate,
        device(z, x, y + 1 - 2 * a, b),
        device(z, x, y + 1 - 2 * a, 1 - b),
        device(zp, x, y, b),
        device(zm, x, y, b),
        device(z, xp, y, b),
        device(z, xm, y, b),
        device(z, xo, y, b),
        device(z, x, yp, b),
        device(z, x, ym, b),
        device(z, x, (shift_src // 2) * 2 + b, shift_src % 2),
    ]
    for other in greet:
        pl.semaphore_signal(bar, inc=1, device_id=other, device_id_type=MESH)
    pl.semaphore_wait(bar, len(greet))

    def remote(src, dst, i, to):
        return pltpu.make_async_remote_copy(
            src_ref=src, dst_ref=dst, send_sem=ssem.at[i], recv_sem=rsem.at[i],
            device_id=to, device_id_type=MESH,
        )

    def send(src, dst, i, to):
        copy = remote(src, dst, i, to)
        copy.start()
        pending.append(copy.wait_send)

    def arrived(dst, i):
        remote(dst, dst, i, mate).wait_recv()

    def send_or_keep(src, dst, i, to, here):
        @pl.when(here)
        def _():
            pltpu.make_async_copy(src, dst, rsem.at[i]).start()

        @pl.when(jnp.logical_not(here))
        def _():
            remote(src, dst, i, to).start()

        def wait():
            @pl.when(jnp.logical_not(here))
            def _():
                remote(src, dst, i, to).wait_send()

        pending.append(wait)

    weights = (wk, wq, wv, wo)
    quad = [take(4) for _ in weights]
    for n, w in enumerate(weights):
        for h in (0, 1):
            src = w.at[:, pl.ds(h * HALF, HALF)]
            dst = W.at[n, z, x, pl.ds(a * 16, 16), :]
            here = jnp.logical_and(a == h, b == h)
            i = quad[n] + 2 * h + a

            @pl.when(here)
            def _():
                pltpu.make_async_copy(src, dst, rsem.at[i]).start()

            @pl.when(jnp.logical_not(here))
            def _():
                remote(src, dst, i, device(z, x, yhi * 2 + b, h)).start()

            def wait(src=src, dst=dst, i=i, h=h, here=here):
                @pl.when(jnp.logical_not(here))
                def _():
                    remote(src, dst, i, device(z, x, yhi * 2 + b, h)).wait_send()

            pending.append(wait)

    gain_mate = take()
    send(gain, GM, gain_mate, mate)

    tok, tok_mate = take(), take()
    send(prev, T.at[a], tok, device(z, x, (yhi * 2 + b + 1) % NY, a))

    def slot(yy, core):
        return E.at[yy % 2, (yy // 2) * 2 + core]

    def half(ref, i):
        return ref.at[pl.ds(i * 128, 128), :]

    e_p, e_m, e_op, e_om = take(2), take(2), take(), take()
    c_own, c_p, c_m, c_o = take(), take(2), take(2), take(2)
    for i in (0, 1):
        send(half(enc, i), half(slot(y, b), i), e_p + i, device(z, x, yp, b))
        send(half(enc, 1 - i), half(slot(y, b), 1 - i), e_m + 1 - i, device(z, x, ym, b))
    own = pltpu.make_async_copy(enc, slot(y, b), rsem.at[take()])
    own.start()
    send(enc, slot(y, b), c_own, mate)

    left, right = pl.ds(0, 256), pl.ds(256, 256)
    ax = [take(3) for _ in weights]
    az = [take(8) for _ in weights]
    bz = [take(8) for _ in weights]
    bx = [take(4) for _ in weights]

    def zz(d):
        return (z + d + NZ) % NZ

    def xx(d):
        return (x + d + NX) % NX

    def a_block(n, zi, xs=None):
        return W.at[n, zi, :, :, left] if xs is None else W.at[n, zi, pl.ds(xs, 2), :, left]

    def b_block(n, zi, rows=None):
        if rows is None:
            return W.at[n, zi, x, :, right]
        return W.at[n, zi, x, pl.ds(rows, 16), right]

    def b_slab(n, xi, zs=None):
        return W.at[n, :, xi, :, right] if zs is None else W.at[n, pl.ds(zs, 4), xi, :, right]

    def ring_z(block, sem, n, step):
        if step > 1:
            arrived(block(n, zz(1 - step)), sem[n] + 2 * (step - 2))
            arrived(block(n, zz(step - 1)), sem[n] + 2 * (step - 2) + 1)
        up, down = device(zp, x, y, b), device(zm, x, y, b)
        i = sem[n] + 2 * (step - 1)
        if step < 4:
            send(block(n, zz(1 - step)), block(n, zz(1 - step)), i, up)
            send(block(n, zz(step - 1)), block(n, zz(step - 1)), i + 1, down)
        else:
            lo, hi = (0, 2) if block is a_block else (0, 16)
            send(block(n, zz(-3), lo), block(n, zz(-3), lo), i, up)
            send(block(n, zz(3), hi), block(n, zz(3), hi), i + 1, down)

    def ring_z_end(block, sem, n):
        lo, hi = (0, 2) if block is a_block else (0, 16)
        arrived(block(n, zz(4), lo), sem[n] + 6)
        arrived(block(n, zz(4), hi), sem[n] + 7)

    def s1(n):
        mine = W.at[n, z, x]
        for i in (0, 1):
            arrived(mine.at[pl.ds(16 * i, 16), :], quad[n] + 2 * b + i)
        piece = W.at[n, z, x, :, left]
        for i, xi in enumerate((xp, xm, xo)):
            send(piece, piece, ax[n] + i, device(z, xi, y, b))
        ring_z(b_block, bz, n, 1)

    def s2(n):
        for i, xi in enumerate((xm, xp, xo)):
            arrived(W.at[n, z, xi, :, left], ax[n] + i)
        ring_z(a_block, az, n, 1)
        ring_z(b_block, bz, n, 2)

    def s3(n):
        ring_z(b_block, bz, n, 3)
        ring_z(a_block, az, n, 2)

    def s4(n):
        ring_z(b_block, bz, n, 4)
        ring_z(a_block, az, n, 3)

    def s5(n):
        ring_z_end(b_block, bz, n)
        send(b_slab(n, x), b_slab(n, x), bx[n], device(z, xp, y, b))
        send(b_slab(n, x), b_slab(n, x), bx[n] + 1, device(z, xm, y, b))
        ring_z(a_block, az, n, 4)

    def s6(n):
        arrived(b_slab(n, xm), bx[n])
        arrived(b_slab(n, xp), bx[n] + 1)
        send(b_slab(n, xm, 0), b_slab(n, xm, 0), bx[n] + 2, device(z, xp, y, b))
        send(b_slab(n, xp, 4), b_slab(n, xp, 4), bx[n] + 3, device(z, xm, y, b))

    def s7(n):
        ring_z_end(a_block, az, n)
        arrived(b_slab(n, xo, 0), bx[n] + 2)
        arrived(b_slab(n, xo, 4), bx[n] + 3)

    def e1():
        arrived(T.at[b], tok)
        send(T.at[b], T.at[b], tok_mate, mate)

    def e2():
        arrived(half(slot(ym, b), 0), e_p)
        send(half(slot(ym, b), 0), half(slot(ym, b), 0), e_op, device(z, x, yp, b))
        send(half(slot(ym, b), 0), half(slot(ym, b), 0), c_m, mate)
        arrived(half(slot(yp, b), 1), e_m + 1)
        send(half(slot(yp, b), 1), half(slot(yp, b), 1), e_om, device(z, x, ym, b))
        send(half(slot(yp, b), 1), half(slot(yp, b), 1), c_p + 1, mate)

    def e3():
        arrived(half(slot(ym, b), 1), e_p + 1)
        send(half(slot(ym, b), 1), half(slot(ym, b), 1), c_m + 1, mate)
        arrived(half(slot(yp, b), 0), e_m)
        send(half(slot(yp, b), 0), half(slot(yp, b), 0), c_p, mate)

    def e4():
        arrived(half(slot(yo, b), 0), e_op)
        send(half(slot(yo, b), 0), half(slot(yo, b), 0), c_o, mate)
        arrived(half(slot(yo, b), 1), e_om)
        send(half(slot(yo, b), 1), half(slot(yo, b), 1), c_o + 1, mate)

    stages = (s1, s2, s3, s4, s5, s6, s7)
    extra = {2: e1, 4: e2, 6: e3, 9: e4}
    for time in range(len(stages) + 3):
        for n in range(4):
            if 0 <= time - n < len(stages):
                stages[time - n](n)
        if time in extra:
            extra[time]()

    own.wait()
    arrived(T.at[1 - b], tok_mate)
    arrived(slot(y, 1 - b), c_own)
    for i in (0, 1):
        arrived(half(slot(ym, 1 - b), i), c_m + i)
        arrived(half(slot(yp, 1 - b), i), c_p + i)
        arrived(half(slot(yo, 1 - b), i), c_o + i)

    def weight(n):
        return W[n].reshape(D, HALF)

    arrived(GM, gain_mate)
    scale = jnp.where(a == b, gain[...], GM[...])
    normed = rms(T[...].reshape(2 * DEC, D).astype(F32), scale).astype(BF)
    Q[...] = dot(normed, weight(1)).astype(BF)

    @pl.loop(0, 8)
    def _(i):
        block = E[i // 4, i % 4]
        K[pl.ds(i * 256, 256), :] = dot(block, weight(0)).astype(BF)
        V[pl.ds(i * 256, 256), :] = dot(block, weight(2)).astype(BF)

    lane = lax.broadcasted_iota(jnp.int32, (DEC, 128), 1)

    @pl.loop(0, 8)
    def _(i):
        seq, pair = i // 4, i % 4
        columns = pl.ds(pl.multiple_of(pair * 128, 128), 128)
        rows = pl.ds(seq * DEC, DEC)
        keys = pl.ds(seq * ENC, ENC)
        q = Q[rows, columns]
        both = jnp.concatenate(
            [jnp.where(lane < 64, q, 0).astype(BF), jnp.where(lane >= 64, q, 0).astype(BF)], axis=0
        )
        scores = lax.dot_general(
            both, K[keys, columns], (((1,), (1,)), ((), ())), preferred_element_type=F32
        )
        top = jnp.max(scores, axis=-1, keepdims=True)
        expo = jnp.exp((scores - top) * 0.125)
        probs = (expo * (1.0 / jnp.sum(expo, axis=-1, keepdims=True))).astype(BF)
        mixed2 = dot(probs, V[keys, columns])
        C[b, rows, columns] = jnp.where(lane < 64, mixed2[:DEC], mixed2[DEC:]).astype(BF)

    ctx = take()
    send(C.at[b], C.at[b], ctx, mate)
    arrived(C.at[1 - b], ctx)
    wout = weight(3)
    attn = dot(C[0], wout[:HALF]) + dot(C[1], wout[HALF:])
    mine = pl.ds(pl.multiple_of(b * HALF, HALF), HALF)
    for c in (0, 1):
        MX[c] = (T[c, :, mine].astype(F32) + attn[c * DEC : (c + 1) * DEC]).astype(BF)

    home = take(4)
    for c in (0, 1):
        src, dst = MX.at[c], H.at[b]
        i = home + 2 * c + b
        here = jnp.logical_and(a == c, b == c)
        to = device(z, x, yhi * 2 + c, a)
        send_or_keep(src, dst, i, to, here)
    for h in (0, 1):
        arrived(H.at[h], home + 2 * a + h)
    for h in (0, 1):
        out[:, h * HALF : (h + 1) * HALF] = H[h]
    for wait in pending:
        wait()


def attention(prev, enc, wq, wk, wv, wo, gain):
    vmem = pl.BlockSpec(memory_space=pltpu.VMEM)
    return pl.pallas_call(
        attention_kernel,
        name="attention",
        out_shape=jax.ShapeDtypeStruct((DEC, D), BF),
        in_specs=[vmem] * 7,
        out_specs=vmem,
        scratch_shapes=[
            pltpu.VMEM((2, 4, 256, D), BF),
            pltpu.VMEM((4, NZ, NX, 32, HALF), BF),
            pltpu.VMEM((2, DEC, D), BF),
            pltpu.VMEM((2 * ENC, HALF), BF),
            pltpu.VMEM((2 * ENC, HALF), BF),
            pltpu.VMEM((2 * DEC, HALF), BF),
            pltpu.VMEM((2, 2 * DEC, HALF), BF),
            pltpu.VMEM((2, DEC, HALF), BF),
            pltpu.VMEM((2, DEC, HALF), BF),
            pltpu.VMEM((1, D), F32),
            pltpu.SemaphoreType.DMA((SEMS_A,)),
            pltpu.SemaphoreType.DMA((SEMS_A,)),
        ],
        compiler_params=pltpu.CompilerParams(
            collective_id=1, has_side_effects=True, vmem_limit_bytes=48 << 20
        ),
    )(prev, enc, wq, wk, wv, wo, gain)


def moe_kernel(mixed, gain, routes, routes_t, gates, spread, gather, wg, wu, wd, out,
               G, U, DN, B0, BUF, X, XR, HID, OWN, PS, PX, RB, R, RR,
               wsem, dsend, drecv, fsend, frecv, psem, rsend, rrecv):
    z, x, y, b = place_of()
    sec, exp = lax.axis_index("section"), lax.axis_index("expert")
    here, a = exp // 2, exp % 2
    partner = (sec, exp + 1 - 2 * a)

    loads = [
        pltpu.make_async_copy(src, dst, wsem.at[i])
        for i, (src, dst) in enumerate(((wg, G), (wu, U), (wd, DN)))
    ]
    for load in loads:
        load.start()

    def at(k, sign):
        zk, xk = k // NX, k % NX
        return ((z + sign * zk + NZ) % NZ) * NX + (x + sign * xk + NX) % NX

    bar = pltpu.get_barrier_semaphore()

    @pl.loop(1, 32)
    def _(k):
        pl.semaphore_signal(bar, inc=1, device_id=(sec, at(k, -1) * 2 + a), device_id_type=MESH)

    pl.semaphore_signal(bar, inc=1, device_id=partner, device_id_type=MESH)

    def remote(src, dst, s, r, to):
        return pltpu.make_async_remote_copy(
            src_ref=src, dst_ref=dst, send_sem=s, recv_sem=r, device_id=to, device_id_type=MESH
        )

    moe_in = rms(mixed[...].astype(F32), gain[...]).astype(BF)
    expert_r = lax.broadcasted_iota(jnp.int32, (EXPERTS, DEC), 0)
    hot = [(expert_r == routes_t[k : k + 1, :]).astype(F32) for k in (0, 1)]
    t0 = lax.broadcasted_iota(jnp.int32, (DEC, DEC), 0)
    t1 = lax.broadcasted_iota(jnp.int32, (DEC, DEC), 1)
    count = dot((hot[0] + hot[1]).astype(BF), (t0 < t1).astype(BF))
    slot_id = lax.broadcasted_iota(jnp.int32, (SLOTS, DEC), 0)
    place = jnp.zeros((SLOTS, DEC), F32)
    for k in (0, 1):
        slot = jnp.sum(count * hot[k], axis=0, keepdims=True).astype(jnp.int32)
        position = routes_t[k : k + 1, :] * CAP + slot
        place = place + (slot_id == position).astype(F32)
    B0[...] = dot(place.astype(BF), moe_in).astype(BF)

    def to_blocks(src, dst):
        @pl.loop(0, 8)
        def _(g):
            rows = pl.ds(g * 48, 48)
            stacked = jnp.concatenate(
                [src[rows, q * QUART : (q + 1) * QUART] for q in range(4)], axis=0
            )
            dst[pl.ds(g * 4, 4)] = dot(spread[...], stacked).astype(BF).reshape(4, 48, QUART)

    def to_rows(src, dst, first):
        @pl.loop(0, 8)
        def _(g):
            stacked = dot(gather[...], src[pl.ds(g * 4, 4)].reshape(192, QUART)).astype(BF)
            for q in range(4):
                dst[pl.ds(first + g * 48, 48), q * QUART : (q + 1) * QUART] = stacked[
                    q * 48 : (q + 1) * 48
                ]

    to_blocks(B0, BUF)
    pl.semaphore_wait(bar, 32)

    @pl.loop(1, 32)
    def _(k):
        to = at(k, 1)
        remote(BUF.at[to], X.at[0, here], dsend.at[k], drecv.at[k], (sec, to * 2 + a)).start()

    X[0, here] = BUF[here]

    @pl.loop(0, 32)
    def _(k):
        src = at(k, -1)

        @pl.when(k > 0)
        def _():
            remote(X.at[0, src], X.at[0, src], dsend.at[k], drecv.at[k], partner).wait_recv()

        remote(X.at[0, src], X.at[1, src], fsend.at[k], frecv.at[k], partner).start()

    @pl.loop(0, 32)
    def _(k):
        src = at(k, -1)
        remote(X.at[1, src], X.at[1, src], fsend.at[k], frecv.at[k], partner).wait()

    to_rows(X.at[0], XR, 0)
    to_rows(X.at[1], XR, SLOTS)
    for load in loads:
        load.wait()

    def expert(first):
        rows = XR[pl.ds(first, 192), :]
        gated, upper = dot(rows, G[...]), dot(rows, U[...])
        HID[...] = (jax.nn.gelu(gated) * upper).astype(BF)
        return dot(HID[...], DN[...])

    @pl.loop(0, 2)
    def _(i):
        PS[pl.ds(i * 192, 192), :] = expert(SLOTS + i * 192).astype(BF)

    swap = remote(PS, PX, psem.at[0], psem.at[1], partner)
    swap.start()

    @pl.loop(0, 2)
    def _(i):
        OWN[pl.ds(i * 192, 192), :] = expert(i * 192)

    swap.wait()
    B0[...] = (OWN[...] + PX[...].astype(F32)).astype(BF)
    to_blocks(B0, RB)

    @pl.loop(1, 32)
    def _(k):
        to = at(k, 1)
        remote(RB.at[to], R.at[here], rsend.at[k], rrecv.at[k], (sec, to * 2 + a)).start()

    R[here] = RB[here]

    expert_c = lax.broadcasted_iota(jnp.int32, (DEC, EXPERTS), 1)
    hot = [(expert_c == routes[:, k : k + 1]).astype(F32) for k in (0, 1)]
    count = dot((t1 < t0).astype(BF), (hot[0] + hot[1]).astype(BF))
    slot_id = lax.broadcasted_iota(jnp.int32, (DEC, SLOTS), 1)
    picks = []
    for k in (0, 1):
        slot = jnp.sum(count * hot[k], axis=1, keepdims=True).astype(jnp.int32)
        picks.append((slot_id == routes[:, k : k + 1] * CAP + slot).astype(F32).astype(BF))

    @pl.loop(1, 32)
    def _(k):
        src = at(k, -1)
        remote(R.at[src], R.at[src], rsend.at[k], rrecv.at[k], partner).wait()
        remote(BUF.at[src], BUF.at[src], dsend.at[k], drecv.at[k], partner).wait_send()

    to_rows(R, RR, 0)
    total = mixed[...].astype(F32)
    moe = [dot(picks[k], RR[...]) * gates[:, k : k + 1] for k in (0, 1)]
    out[...] = (total + (moe[0] + moe[1])).astype(BF)


def spread_matrix():
    m = np.zeros((192, 192), np.float32)
    for s in range(4):
        for q in range(4):
            for c in range(CAP):
                m[s * 48 + q * 12 + c, q * 48 + s * 12 + c] = 1
    return m


def experts(mixed, gain, routes, gates, wg, wu, wd):
    vmem, hbm = pl.BlockSpec(memory_space=pltpu.VMEM), pl.BlockSpec(memory_space=pl.ANY)
    spread = spread_matrix()
    dma = pltpu.SemaphoreType.DMA
    return pl.pallas_call(
        moe_kernel,
        name="experts",
        out_shape=jax.ShapeDtypeStruct((DEC, D), BF),
        in_specs=[vmem] * 7 + [hbm] * 3,
        out_specs=vmem,
        scratch_shapes=[
            pltpu.VMEM((D, PIECE), BF),
            pltpu.VMEM((D, PIECE), BF),
            pltpu.VMEM((PIECE, D), BF),
            pltpu.VMEM((SLOTS, D), BF),
            pltpu.VMEM((32, 48, QUART), BF),
            pltpu.VMEM((2, 32, 48, QUART), BF),
            pltpu.VMEM((2 * SLOTS, D), BF),
            pltpu.VMEM((192, PIECE), BF),
            pltpu.VMEM((SLOTS, D), F32),
            pltpu.VMEM((SLOTS, D), BF),
            pltpu.VMEM((SLOTS, D), BF),
            pltpu.VMEM((32, 48, QUART), BF),
            pltpu.VMEM((32, 48, QUART), BF),
            pltpu.VMEM((SLOTS, D), BF),
            dma((3,)),
            dma((32,)),
            dma((32,)),
            dma((32,)),
            dma((32,)),
            dma((2,)),
            dma((32,)),
            dma((32,)),
        ],
        compiler_params=pltpu.CompilerParams(
            collective_id=2, has_side_effects=True, vmem_limit_bytes=56 << 20
        ),
    )(mixed, gain, routes, routes.T, gates, jnp.asarray(spread, BF), jnp.asarray(spread.T, BF), wg, wu, wd)


def per_device(previous, encoder_states, routes, gate_values, gain_attn, gain_moe, query_weight,
               key_weight, value_weight, out_weight, expert_gate, expert_up, expert_down):
    mixed = attention(
        previous[0, 0], encoder_states[0], query_weight[0], key_weight[0], value_weight[0],
        out_weight[0], gain_attn,
    )
    result = experts(
        mixed, gain_moe, routes[0, 0], gate_values[0, 0], expert_gate[0, 0], expert_up[0, 0],
        expert_down[0, 0],
    )
    return result.reshape(previous.shape)


def solution(mesh):
    in_specs = (
        P("section", "expert", None, None),
        P("expert", "section", None),
        P("section", "expert", None, None),
        P("section", "expert", None, None),
        P("section", None),
        P("section", None),
        P("section", "expert", None),
        P("section", "expert", None),
        P("section", "expert", None),
        P("section", "expert", None),
        P("section", "expert", None, None),
        P("section", "expert", None, None),
        P("section", "expert", None, None),
    )
    out_specs = P("section", "expert", None, None)
    return jax.shard_map(
        per_device, mesh=mesh, in_specs=in_specs, out_specs=out_specs, check_vma=False
    )
```

```python
import functools

import jax
import jax.numpy as jnp
import numpy as np
from jax import lax
from jax.experimental import pallas as pl
from jax.experimental.pallas import tpu as pltpu
from jax.sharding import PartitionSpec as P

EXPERTS = 32
CAP = 12
NZ, NX, NY = 8, 4, 4
DEC, ENC, D = 128, 1024, 1024
HALF = D // 2
QUART = D // 4
PIECE = 1408
SLOTS = EXPERTS * CAP
EPS = 1e-06
MESH = pl.DeviceIdType.MESH
BF, F32 = jnp.bfloat16, jnp.float32


def place_of():
    s, e = lax.axis_index("section"), lax.axis_index("expert")
    return e // 8, (e // 2) % NX, (s // 2) * 2 + e % 2, s % 2


def device(z, x, y, core):
    return ((y // 2) * 2 + core, (z * NX + x) * 2 + y % 2)


class Sems:
    def __init__(self, ref):
        self.ref, self.used = ref, 0

    def take(self, count=1):
        first = self.used
        self.used += count
        return first


def rms(x, gain):
    return x * lax.rsqrt(jnp.mean(x * x, axis=-1, keepdims=True) + EPS) * gain


def dot(a, b):
    return jnp.dot(a, b, preferred_element_type=F32)


SEMS_A = 180


GROUPS = (
    (
        (("k", 0), ("k", 1), ("v", 0), ("v", 1), ("q", 0), ("q", 1)),
        (("k", 2), ("k", 3), ("v", 2), ("v", 3), ("q", 2), ("q", 3)),
    ),
    (
        (("o", 0),),
        (("o", 1), ("o", 2), ("o", 3)),
    ),
)


def make_plan(behind, places):
    plan = []
    for time in range(1, 9 + behind):
        plan += [f"s{time - g * behind} {g}" for g in (0, 1) if 1 <= time - g * behind <= 8]
        plan += places.get(time, [])
    return plan + places.get(0, [])


PLAN = make_plan(
    2,
    {
        5: ["e2"],
        7: ["e3", "e1"],
        8: ["e4", "ck 0", "ck 1"],
        9: ["ck 3", "ck 2", "cv 0", "cv 1", "cv 3", "cv 2", "cq", "at 0"],
        10: ["at 1"],
    },
)


def attention_kernel(plan, prev, enc, wq, wk, wv, wo, gain, out, E, WA0, WB0, WA1, WB1, T, K, V, Q, C, MX, H, GM, GO, S, ssem, rsem):
    WA, WB = (WA0, WA1), (WB0, WB1)
    z, x, y, b = place_of()
    a, yhi = y % 2, y // 2
    zp, zm = (z + 1) % NZ, (z + NZ - 1) % NZ
    xp, xm, xo = (x + 1) % NX, (x + NX - 1) % NX, (x + 2) % NX
    yp, ym, yo = (y + 1) % NY, (y + NY - 1) % NY, (y + 2) % NY
    mate = device(z, x, y, 1 - b)
    take = Sems(rsem).take
    pending = []

    bar = pltpu.get_barrier_semaphore()
    shift_src = (y + 3) % NY
    greet = [
        mate,
        device(z, x, y + 1 - 2 * a, b),
        device(z, x, y + 1 - 2 * a, 1 - b),
        device(zp, x, y, b),
        device(zm, x, y, b),
        device(z, xp, y, b),
        device(z, xm, y, b),
        device(z, xo, y, b),
        device(z, x, yp, b),
        device(z, x, ym, b),
        device(z, x, (shift_src // 2) * 2 + b, shift_src % 2),
    ]
    for other in greet:
        pl.semaphore_signal(bar, inc=1, device_id=other, device_id_type=MESH)
    pl.semaphore_wait(bar, len(greet))

    def remote(src, dst, i, to):
        return pltpu.make_async_remote_copy(
            src_ref=src, dst_ref=dst, send_sem=ssem.at[i], recv_sem=rsem.at[i],
            device_id=to, device_id_type=MESH,
        )

    def send(src, dst, i, to):
        copy = remote(src, dst, i, to)
        copy.start()
        pending.append(copy.wait_send)

    def arrived(dst, i):
        remote(dst, dst, i, mate).wait_recv()

    def send_or_keep(src, dst, i, to, here):
        @pl.when(here)
        def _():
            pltpu.make_async_copy(src, dst, rsem.at[i]).start()

        @pl.when(jnp.logical_not(here))
        def _():
            remote(src, dst, i, to).start()

        def wait():
            @pl.when(jnp.logical_not(here))
            def _():
                remote(src, dst, i, to).wait_send()

        pending.append(wait)

    names = "kvqo"
    weights = dict(k=wk, v=wv, q=wq, o=wo)
    quad = [take(4) for _ in names]
    for n, name in enumerate(names):
        for h in (0, 1):
            send_or_keep(
                weights[name].at[:, pl.ds(h * HALF, HALF)], S.at[n, a], quad[n] + 2 * h + a,
                device(z, x, yhi * 2 + b, h), jnp.logical_and(a == h, b == h),
            )

    gain_mate = take()
    send(gain, GM, gain_mate, mate)
    gain_in = pltpu.make_async_copy(gain, GO, rsem.at[take()])
    gain_in.start()

    def slot(yy, core):
        return E.at[yy % 2, (yy // 2) * 2 + core]

    def half(ref, i):
        return ref.at[pl.ds(i * 128, 128), :]

    e_p, e_m, e_op, e_om = take(2), take(2), take(), take()
    c_own, c_p, c_m, c_o = take(), take(2), take(2), take(2)
    for i in (0, 1):
        send(half(enc, i), half(slot(y, b), i), e_p + i, device(z, x, yp, b))
        send(half(enc, 1 - i), half(slot(y, b), 1 - i), e_m + 1 - i, device(z, x, ym, b))
    tok, tok_mate = take(), take()
    send(prev, T.at[a], tok, device(z, x, (yhi * 2 + b + 1) % NY, a))

    own = pltpu.make_async_copy(enc, slot(y, b), rsem.at[take()])
    own.start()
    send(enc, slot(y, b), c_own, mate)

    ax, az, bz, bx, bo = ([take(m) for _ in GROUPS] for m in (3, 8, 8, 16, 8))
    up, down = device(zp, x, y, b), device(zm, x, y, b)
    east, west = device(z, xp, y, b), device(z, xm, y, b)

    def zz(d):
        return (z + d + NZ) % NZ

    def pass_on(ref, i, to):
        send(ref, ref, i, to)

    def a_ring(g, step):
        ref, i = WA[g], az[g] + 2 * (step - 1)
        if step > 1:
            arrived(ref.at[zz(1 - step)], i - 2)
            arrived(ref.at[zz(step - 1)], i - 1)
        if step < 4:
            pass_on(ref.at[zz(1 - step)], i, up)
            pass_on(ref.at[zz(step - 1)], i + 1, down)
        else:
            pass_on(ref.at[zz(-3), pl.ds(0, 2)], i, up)
            pass_on(ref.at[zz(3), pl.ds(2, 2)], i + 1, down)

    def a_end(g):
        arrived(WA[g].at[zz(4), pl.ds(0, 2)], az[g] + 6)
        arrived(WA[g].at[zz(4), pl.ds(2, 2)], az[g] + 7)

    def b_ring(g, step):
        ref, i = WB[g].at[x], bz[g] + 2 * (step - 1)
        if step > 1:
            arrived(ref.at[zz(1 - step)], i - 2)
            arrived(ref.at[zz(step - 1)], i - 1)
        if step < 4:
            pass_on(ref.at[zz(1 - step)], i, up)
            pass_on(ref.at[zz(step - 1)], i + 1, down)
        else:
            pass_on(ref.at[zz(-3), :, pl.ds(0, 16), :], i, up)
            pass_on(ref.at[zz(3), :, pl.ds(16, 16), :], i + 1, down)

    def b_end(g):
        arrived(WB[g].at[x, zz(4), :, pl.ds(0, 16), :], bz[g] + 6)
        arrived(WB[g].at[x, zz(4), :, pl.ds(16, 16), :], bz[g] + 7)

    def b_out(g, *steps):
        for d in steps:
            block = WB[g].at[x, zz(d)]
            pass_on(block, bx[g] + 2 * (d % 8), east)
            pass_on(block, bx[g] + 2 * (d % 8) + 1, west)

    def b_on(g, *steps):
        for d in steps:
            arrived(WB[g].at[xm, zz(d)], bx[g] + 2 * (d % 8))
            arrived(WB[g].at[xp, zz(d)], bx[g] + 2 * (d % 8) + 1)
            if d <= 0:
                pass_on(WB[g].at[xm, zz(d)], bo[g] + d % 8, east)
            else:
                pass_on(WB[g].at[xp, zz(d)], bo[g] + d % 8, west)

    def b_far(g):
        for d in range(-3, 5):
            arrived(WB[g].at[xo, zz(d)], bo[g] + d % 8)

    def s1(g):
        used = sorted({w for units in GROUPS[g] for w, _ in units})
        for w in used:
            for i in (0, 1):
                arrived(S.at[names.index(w), i], quad[names.index(w)] + 2 * b + i)
        for path, units in enumerate(GROUPS[g]):
            for n, (w, u) in enumerate(units):
                unit = S[names.index(w), :, :, u * 128 : (u + 1) * 128].reshape(32, 128)
                if path == 0:
                    WA[g][z, x, n] = unit
                else:
                    WB[g][x, z, n] = unit
        b_ring(g, 1)
        for i, xi in enumerate((xp, xm, xo)):
            send(WA[g].at[z, x], WA[g].at[z, x], ax[g] + i, device(z, xi, y, b))
        b_out(g, 0)

    def s2(g):
        b_ring(g, 2)
        b_out(g, -1, 1)
        for i, xi in enumerate((xm, xp, xo)):
            arrived(WA[g].at[z, xi], ax[g] + i)
        a_ring(g, 1)

    def s3(g):
        b_ring(g, 3)
        b_out(g, -2, 2)
        b_on(g, 0)

    def s4(g):
        b_ring(g, 4)
        b_out(g, -3, 3)
        a_ring(g, 2)
        b_on(g, -1, 1)

    def s5(g):
        b_end(g)
        b_out(g, 4)
        b_on(g, -2, 2)

    def s6(g):
        a_ring(g, 3)
        b_on(g, -3, 3)

    def s7(g):
        a_ring(g, 4)
        b_on(g, 4)

    def s8(g):
        a_end(g)
        b_far(g)

    def e1():
        arrived(T.at[b], tok)
        send(T.at[b], T.at[b], tok_mate, mate)

    def e2():
        arrived(half(slot(ym, b), 0), e_p)
        send(half(slot(ym, b), 0), half(slot(ym, b), 0), e_op, device(z, x, yp, b))
        send(half(slot(ym, b), 0), half(slot(ym, b), 0), c_m, mate)
        arrived(half(slot(yp, b), 1), e_m + 1)
        send(half(slot(yp, b), 1), half(slot(yp, b), 1), e_om, device(z, x, ym, b))
        send(half(slot(yp, b), 1), half(slot(yp, b), 1), c_p + 1, mate)

    def e3():
        arrived(half(slot(ym, b), 1), e_p + 1)
        send(half(slot(ym, b), 1), half(slot(ym, b), 1), c_m + 1, mate)
        arrived(half(slot(yp, b), 0), e_m)
        send(half(slot(yp, b), 0), half(slot(yp, b), 0), c_p, mate)

    def e4():
        arrived(half(slot(yo, b), 0), e_op)
        send(half(slot(yo, b), 0), half(slot(yo, b), 0), c_o, mate)
        arrived(half(slot(yo, b), 1), e_om)
        send(half(slot(yo, b), 1), half(slot(yo, b), 1), c_o + 1, mate)

    def weight(w):
        units = []
        for u in range(4):
            for g, paths in enumerate(GROUPS):
                if (w, u) in paths[0]:
                    units.append(WA[g][:, :, paths[0].index((w, u))].reshape(D, 128))
                if (w, u) in paths[1]:
                    unit = WB[g][:, :, paths[1].index((w, u))]
                    units.append(jnp.swapaxes(unit, 0, 1).reshape(D, 128))
        return jnp.concatenate(units, axis=1)

    def cq():
        arrived(T.at[1 - b], tok_mate)
        arrived(GM, gain_mate)
        gain_in.wait()
        scale = jnp.where(a == b, GO[...], GM[...])
        normed = rms(T[...].reshape(2 * DEC, D).astype(F32), scale).astype(BF)
        Q[...] = dot(normed, weight("q")).astype(BF)

    def states(step):
        yy = (y + step) % NY
        return [
            (
                E[yy % 2, (yy // 2) * 2 + core],
                pl.ds(pl.multiple_of((yy % 2) * ENC + ((yy // 2) * 2 + core) * 256, 256), 256),
            )
            for core in (0, 1)
        ]

    def ready(step):
        if step == 0:
            own.wait()
            arrived(slot(y, 1 - b), c_own)
            return
        yy, sem = {1: (yp, c_p), 3: (ym, c_m), 2: (yo, c_o)}[step]
        for i in (0, 1):
            arrived(half(slot(yy, 1 - b), i), sem + i)

    def ck(step):
        ready(step)
        for block, rows in states(step):
            K[rows, :] = dot(block, weight("k")).astype(BF)

    def cv(step):
        for block, rows in states(step):
            V[rows, :] = dot(block, weight("v")).astype(BF)

    lane = lax.broadcasted_iota(jnp.int32, (DEC, 128), 1)

    def at(seq):
        @pl.loop(0, 4)
        def _(pair):
            columns = pl.ds(pl.multiple_of(pair * 128, 128), 128)
            rows = pl.ds(seq * DEC, DEC)
            keys = pl.ds(seq * ENC, ENC)
            q = Q[rows, columns]
            both = jnp.concatenate(
                [jnp.where(lane < 64, q, 0).astype(BF), jnp.where(lane >= 64, q, 0).astype(BF)],
                axis=0,
            )
            scores = lax.dot_general(
                both, K[keys, columns], (((1,), (1,)), ((), ())), preferred_element_type=F32
            )
            top = jnp.max(scores, axis=-1, keepdims=True)
            expo = jnp.exp((scores - top) * 0.125)
            probs = (expo * (1.0 / jnp.sum(expo, axis=-1, keepdims=True))).astype(BF)
            mixed2 = dot(probs, V[keys, columns])
            C[b, rows, columns] = jnp.where(lane < 64, mixed2[:DEC], mixed2[DEC:]).astype(BF)

    ops = dict(s1=s1, s2=s2, s3=s3, s4=s4, s5=s5, s6=s6, s7=s7, s8=s8, e1=e1, e2=e2, e3=e3, e4=e4,
               cq=cq, ck=ck, cv=cv, at=at, rd=ready)
    for op in plan:
        name, _, arg = op.partition(" ")
        ops[name](*([int(arg)] if arg else []))

    ctx = take()
    send(C.at[b], C.at[b], ctx, mate)
    arrived(C.at[1 - b], ctx)
    wout = weight("o")
    attn = dot(C[0], wout[:HALF]) + dot(C[1], wout[HALF:])
    mine = pl.ds(pl.multiple_of(b * HALF, HALF), HALF)
    for c in (0, 1):
        MX[c] = (T[c, :, mine].astype(F32) + attn[c * DEC : (c + 1) * DEC]).astype(BF)

    home = take(4)
    for c in (0, 1):
        src, dst = MX.at[c], H.at[b]
        i = home + 2 * c + b
        here = jnp.logical_and(a == c, b == c)
        to = device(z, x, yhi * 2 + c, a)
        send_or_keep(src, dst, i, to, here)
    for h in (0, 1):
        arrived(H.at[h], home + 2 * a + h)
    for h in (0, 1):
        out[:, h * HALF : (h + 1) * HALF] = H[h]
    for wait in pending:
        wait()


def attention(prev, enc, wq, wk, wv, wo, gain):
    vmem = pl.BlockSpec(memory_space=pltpu.VMEM)
    return pl.pallas_call(
        functools.partial(attention_kernel, PLAN),
        name="attention",
        out_shape=jax.ShapeDtypeStruct((DEC, D), BF),
        in_specs=[pl.BlockSpec(memory_space=pl.ANY)] * 7,
        out_specs=vmem,
        scratch_shapes=[
            pltpu.VMEM((2, 4, 256, D), BF),
            pltpu.VMEM((NZ, NX, len(GROUPS[0][0]), 32, 128), BF),
            pltpu.VMEM((NX, NZ, len(GROUPS[0][1]), 32, 128), BF),
            pltpu.VMEM((NZ, NX, len(GROUPS[1][0]), 32, 128), BF),
            pltpu.VMEM((NX, NZ, len(GROUPS[1][1]), 32, 128), BF),
            pltpu.VMEM((2, DEC, D), BF),
            pltpu.VMEM((2 * ENC, HALF), BF),
            pltpu.VMEM((2 * ENC, HALF), BF),
            pltpu.VMEM((2 * DEC, HALF), BF),
            pltpu.VMEM((2, 2 * DEC, HALF), BF),
            pltpu.VMEM((2, DEC, HALF), BF),
            pltpu.VMEM((2, DEC, HALF), BF),
            pltpu.VMEM((1, D), F32),
            pltpu.VMEM((1, D), F32),
            pltpu.VMEM((4, 2, 16, HALF), BF),
            pltpu.SemaphoreType.DMA((SEMS_A,)),
            pltpu.SemaphoreType.DMA((SEMS_A,)),
        ],
        compiler_params=pltpu.CompilerParams(
            collective_id=1, has_side_effects=True, vmem_limit_bytes=48 << 20
        ),
    )(prev, enc, wq, wk, wv, wo, gain)


CHUNKS = ((1, 5), (3, 7), (2, 6), (0, 4))


def moe_kernel(mixed, gain, routes, routes_t, gates, spread, gather, wg, wu, wd, out,
               G, U, DN, B0, BUF, X, XR, HID, OWN, PS, PX, RB, R, RR,
               wsem, dsend, drecv, fsend, frecv, psend, precv, rsend, rrecv):
    z, x, y, b = place_of()
    sec, exp = lax.axis_index("section"), lax.axis_index("expert")
    here, a = exp // 2, exp % 2
    partner = (sec, exp + 1 - 2 * a)

    loads = [
        pltpu.make_async_copy(src, dst, wsem.at[i])
        for i, (src, dst) in enumerate(((wg, G), (wu, U), (wd, DN)))
    ]
    for load in loads:
        load.start()

    def zt(zk, sign):
        return (z + sign * zk + NZ) % NZ

    def xt(xk, sign):
        return (x + sign * xk + NX) % NX

    def plane(zi, xi):
        return (sec, (zi * NX + xi) * 2 + a)

    bar = pltpu.get_barrier_semaphore()

    @pl.loop(1, 32)
    def _(k):
        pl.semaphore_signal(
            bar, inc=1, device_id=plane(zt(k // NX, -1), xt(k % NX, -1)), device_id_type=MESH
        )

    pl.semaphore_signal(bar, inc=1, device_id=partner, device_id_type=MESH)

    def remote(src, dst, s, r, to):
        return pltpu.make_async_remote_copy(
            src_ref=src, dst_ref=dst, send_sem=s, recv_sem=r, device_id=to, device_id_type=MESH
        )

    def to_blocks(rows):
        stacked = jnp.concatenate([rows[:, q * QUART : (q + 1) * QUART] for q in range(4)], axis=0)
        return dot(spread[...], stacked).astype(BF).reshape(4, 48, QUART)

    def to_rows(blocks, dst, first):
        stacked = dot(gather[...], blocks.reshape(192, QUART)).astype(BF)
        for q in range(4):
            dst[pl.ds(first, 48), q * QUART : (q + 1) * QUART] = stacked[q * 48 : (q + 1) * 48]

    moe_in = rms(mixed[...].astype(F32), gain[...]).astype(BF)
    expert_r = lax.broadcasted_iota(jnp.int32, (EXPERTS, DEC), 0)
    hot = [(expert_r == routes_t[k : k + 1, :]).astype(F32) for k in (0, 1)]
    t0 = lax.broadcasted_iota(jnp.int32, (DEC, DEC), 0)
    t1 = lax.broadcasted_iota(jnp.int32, (DEC, DEC), 1)
    count = dot((hot[0] + hot[1]).astype(BF), (t0 < t1).astype(BF))
    slot_id = lax.broadcasted_iota(jnp.int32, (SLOTS, DEC), 0)
    place = jnp.zeros((SLOTS, DEC), F32)
    for k in (0, 1):
        slot = jnp.sum(count * hot[k], axis=0, keepdims=True).astype(jnp.int32)
        position = routes_t[k : k + 1, :] * CAP + slot
        place = place + (slot_id == position).astype(F32)
    B0[...] = dot(place.astype(BF), moe_in).astype(BF)
    pl.semaphore_wait(bar, 32)

    def rows_of(zi):
        return pl.ds(pl.multiple_of(zi * 48, 16), 48)

    def exchange(zi, first, zk, src, dst, s, r, sign):
        @pl.loop(first, NX)
        def _(xk):
            xi = xt(xk, sign)
            k = zk * NX + xk
            remote(src.at[zi * NX + xi], dst.at[here], s.at[k], r.at[k], plane(zi, xi)).start()

    for chunk in CHUNKS:
        for zk in chunk:
            zi = zt(zk, 1)
            BUF[pl.ds(zi * NX, NX)] = to_blocks(B0[rows_of(zi), :])
            exchange(zi, int(zk == 0), zk, BUF, X.at[0], dsend, drecv, 1)
    X[0, here] = BUF[here]

    def group(ref, zk):
        return ref.at[pl.ds(zt(zk, -1) * NX, NX)]

    def forward(chunk):
        for zk in chunk:
            zi = zt(zk, -1)

            @pl.loop(int(zk == 0), NX)
            def _(xk):
                src = X.at[0, zi * NX + xt(xk, -1)]
                remote(src, src, dsend.at[zk * NX + xk], drecv.at[zk * NX + xk], partner).wait_recv()

            remote(group(X.at[0], zk), group(X.at[1], zk), fsend.at[zk], frecv.at[zk], partner).start()

    def swap(j):
        return remote(PS.at[j], PX.at[j], psend.at[j], precv.at[j], partner)

    def work(j, chunk):
        for i, zk in enumerate(chunk):
            remote(group(X.at[1], zk), group(X.at[1], zk), fsend.at[zk], frecv.at[zk], partner).wait_recv()
            to_rows(group(X.at[0], zk)[...], XR, i * 48)
            to_rows(group(X.at[1], zk)[...], XR, 96 + i * 48)
        if j == 0:
            for load in loads:
                load.wait()
        rows = XR[...]
        gated, upper = dot(rows, G[...]), dot(rows, U[...])
        HID[...] = (jax.nn.gelu(gated) * upper).astype(BF)
        PS[j] = dot(HID[96:, :], DN[...]).astype(BF)
        swap(j).start()
        OWN[j] = dot(HID[:96, :], DN[...])

    def back(j, chunk):
        swap(j).wait()
        total = (OWN[j] + PX[j].astype(F32)).astype(BF)
        for i, zk in enumerate(chunk):
            zi = zt(zk, -1)
            RB[pl.ds(zi * NX, NX)] = to_blocks(total[i * 48 : (i + 1) * 48])
            exchange(zi, int(zk == 0), zk, RB, R, rsend, rrecv, -1)
            if zk == 0:
                R[here] = RB[here]

    for j in range(len(CHUNKS) + 2):
        if j < len(CHUNKS):
            forward(CHUNKS[j])
        if 1 <= j <= len(CHUNKS):
            work(j - 1, CHUNKS[j - 1])
        if j >= 2:
            back(j - 2, CHUNKS[j - 2])

    expert_c = lax.broadcasted_iota(jnp.int32, (DEC, EXPERTS), 1)
    hot = [(expert_c == routes[:, k : k + 1]).astype(F32) for k in (0, 1)]
    count = dot((t1 < t0).astype(BF), (hot[0] + hot[1]).astype(BF))
    slot_id = lax.broadcasted_iota(jnp.int32, (DEC, SLOTS), 1)
    picks = []
    for k in (0, 1):
        slot = jnp.sum(count * hot[k], axis=1, keepdims=True).astype(jnp.int32)
        picks.append((slot_id == routes[:, k : k + 1] * CAP + slot).astype(F32).astype(BF))

    for chunk in CHUNKS:
        for zk in chunk:
            zi = zt(zk, 1)
            remote(group(X.at[0], zk), group(X.at[0], zk), fsend.at[zk], frecv.at[zk], partner).wait_send()

            @pl.loop(int(zk == 0), NX)
            def _(xk):
                k = zk * NX + xk
                block = R.at[zi * NX + xt(xk, 1)]
                remote(block, block, rsend.at[k], rrecv.at[k], partner).wait()
                remote(block, block, dsend.at[k], drecv.at[k], partner).wait_send()

            to_rows(R[pl.ds(zi * NX, NX)], RR, pl.multiple_of(zi * 48, 16))
    total = mixed[...].astype(F32)
    moe = [dot(picks[k], RR[...]) * gates[:, k : k + 1] for k in (0, 1)]
    out[...] = (total + (moe[0] + moe[1])).astype(BF)


def spread_matrix():
    m = np.zeros((192, 192), np.float32)
    for s in range(4):
        for q in range(4):
            for c in range(CAP):
                m[s * 48 + q * 12 + c, q * 48 + s * 12 + c] = 1
    return m


def experts(mixed, gain, routes, gates, wg, wu, wd):
    vmem, hbm = pl.BlockSpec(memory_space=pltpu.VMEM), pl.BlockSpec(memory_space=pl.ANY)
    spread = spread_matrix()
    dma = pltpu.SemaphoreType.DMA
    return pl.pallas_call(
        moe_kernel,
        name="experts",
        out_shape=jax.ShapeDtypeStruct((DEC, D), BF),
        in_specs=[vmem] * 7 + [hbm] * 3,
        out_specs=vmem,
        scratch_shapes=[
            pltpu.VMEM((D, PIECE), BF),
            pltpu.VMEM((D, PIECE), BF),
            pltpu.VMEM((PIECE, D), BF),
            pltpu.VMEM((SLOTS, D), BF),
            pltpu.VMEM((32, 48, QUART), BF),
            pltpu.VMEM((2, 32, 48, QUART), BF),
            pltpu.VMEM((192, D), BF),
            pltpu.VMEM((192, PIECE), BF),
            pltpu.VMEM((4, 96, D), F32),
            pltpu.VMEM((4, 96, D), BF),
            pltpu.VMEM((4, 96, D), BF),
            pltpu.VMEM((32, 48, QUART), BF),
            pltpu.VMEM((32, 48, QUART), BF),
            pltpu.VMEM((SLOTS, D), BF),
            dma((3,)),
            dma((32,)),
            dma((32,)),
            dma((8,)),
            dma((8,)),
            dma((4,)),
            dma((4,)),
            dma((32,)),
            dma((32,)),
        ],
        compiler_params=pltpu.CompilerParams(
            collective_id=2, has_side_effects=True, vmem_limit_bytes=56 << 20
        ),
    )(mixed, gain, routes, routes.T, gates, jnp.asarray(spread, BF), jnp.asarray(spread.T, BF), wg, wu, wd)


def per_device(previous, encoder_states, routes, gate_values, gain_attn, gain_moe, query_weight,
               key_weight, value_weight, out_weight, expert_gate, expert_up, expert_down):
    mixed = attention(
        previous[0, 0], encoder_states[0], query_weight[0], key_weight[0], value_weight[0],
        out_weight[0], gain_attn,
    )
    result = experts(
        mixed, gain_moe, routes[0, 0], gate_values[0, 0], expert_gate[0, 0], expert_up[0, 0],
        expert_down[0, 0],
    )
    return result.reshape(previous.shape)


def solution(mesh):
    in_specs = (
        P("section", "expert", None, None),
        P("expert", "section", None),
        P("section", "expert", None, None),
        P("section", "expert", None, None),
        P("section", None),
        P("section", None),
        P("section", "expert", None),
        P("section", "expert", None),
        P("section", "expert", None),
        P("section", "expert", None),
        P("section", "expert", None, None),
        P("section", "expert", None, None),
        P("section", "expert", None, None),
    )
    out_specs = P("section", "expert", None, None)
    return jax.shard_map(
        per_device, mesh=mesh, in_specs=in_specs, out_specs=out_specs, check_vma=False
    )
```

```python
import functools

import jax
import jax.numpy as jnp
from jax import lax
from jax.experimental import pallas as pl
from jax.experimental.pallas import tpu as pltpu
from jax.sharding import PartitionSpec as P

EXPERTS = 32
CAP = 12
NZ, NX, NY = 8, 4, 4
DEC, ENC, D = 128, 1024, 1024
HALF = D // 2
QUART = D // 4
PIECE = 1408
SLOTS = EXPERTS * CAP
EPS = 1e-06
MESH = pl.DeviceIdType.MESH
BF, F32 = jnp.bfloat16, jnp.float32


def place_of():
    s, e = lax.axis_index("section"), lax.axis_index("expert")
    return e // 8, (e // 2) % NX, (s // 2) * 2 + e % 2, s % 2


def device(z, x, y, core):
    return ((y // 2) * 2 + core, (z * NX + x) * 2 + y % 2)


class Sems:
    def __init__(self, ref):
        self.ref, self.used = ref, 0

    def take(self, count=1):
        first = self.used
        self.used += count
        return first


def rms(x, gain):
    return x * lax.rsqrt(jnp.mean(x * x, axis=-1, keepdims=True) + EPS) * gain


def dot(a, b):
    return jnp.dot(a, b, preferred_element_type=F32)


SEMS_A = 180


GROUPS = (
    (
        (("k", 0), ("k", 1), ("v", 0), ("v", 1), ("q", 0), ("q", 1)),
        (("k", 2), ("k", 3), ("v", 2), ("v", 3), ("q", 2), ("q", 3)),
    ),
    (
        (("o", 0),),
        (("o", 1), ("o", 2), ("o", 3)),
    ),
)


def make_plan(behind, places):
    plan = []
    for time in range(1, 9 + behind):
        plan += [f"s{time - g * behind} {g}" for g in (0, 1) if 1 <= time - g * behind <= 8]
        plan += places.get(time, [])
    return plan + places.get(0, [])


PLAN = make_plan(
    2,
    {
        5: ["e2"],
        7: ["e3", "e1"],
        8: ["e4", "ck 0", "ck 1"],
        6: ["ld"],
        9: ["ck 3", "ck 2", "cv 0", "cv 1", "cv 3", "cv 2", "cq", "at 0", "cx 0"],
        10: ["at 1", "cx 1", "op 0", "op 1", "hm"],
    },
)


def attention_part(plan, prev, enc, wq, wk, wv, wo, gain, E, WA0, WB0, WA1, WB1, T, K, V, Q, C, MX, H,
                   GM, GO, S, ssem, rsem, load):
    WA, WB = (WA0, WA1), (WB0, WB1)
    z, x, y, b = place_of()
    a, yhi = y % 2, y // 2
    zp, zm = (z + 1) % NZ, (z + NZ - 1) % NZ
    xp, xm, xo = (x + 1) % NX, (x + NX - 1) % NX, (x + 2) % NX
    yp, ym, yo = (y + 1) % NY, (y + NY - 1) % NY, (y + 2) % NY
    mate = device(z, x, y, 1 - b)
    take = Sems(rsem).take
    pending = []

    bar = pltpu.get_barrier_semaphore()
    shift_src = (y + 3) % NY
    greet = [
        mate,
        device(z, x, y + 1 - 2 * a, b),
        device(z, x, y + 1 - 2 * a, 1 - b),
        device(zp, x, y, b),
        device(zm, x, y, b),
        device(z, xp, y, b),
        device(z, xm, y, b),
        device(z, xo, y, b),
        device(z, x, yp, b),
        device(z, x, ym, b),
        device(z, x, (shift_src // 2) * 2 + b, shift_src % 2),
    ]
    for other in greet:
        pl.semaphore_signal(bar, inc=1, device_id=other, device_id_type=MESH)

    @pl.loop(1, 32)
    def _(k):
        zi, xi = (z + k // NX) % NZ, (x + k % NX) % NX
        pl.semaphore_signal(bar, inc=1, device_id=device(zi, xi, y, b), device_id_type=MESH)

    pl.semaphore_wait(bar, len(greet) + 31)

    def remote(src, dst, i, to):
        return pltpu.make_async_remote_copy(
            src_ref=src, dst_ref=dst, send_sem=ssem.at[i], recv_sem=rsem.at[i],
            device_id=to, device_id_type=MESH,
        )

    def send(src, dst, i, to):
        copy = remote(src, dst, i, to)
        copy.start()
        pending.append(copy.wait_send)

    def arrived(dst, i):
        remote(dst, dst, i, mate).wait_recv()

    def send_or_keep(src, dst, i, to, here):
        @pl.when(here)
        def _():
            pltpu.make_async_copy(src, dst, rsem.at[i]).start()

        @pl.when(jnp.logical_not(here))
        def _():
            remote(src, dst, i, to).start()

        def wait():
            @pl.when(jnp.logical_not(here))
            def _():
                remote(src, dst, i, to).wait_send()

        pending.append(wait)

    names = "kvqo"
    weights = dict(k=wk, v=wv, q=wq, o=wo)
    quad = [take(4) for _ in names]
    for n, name in enumerate(names):
        for h in (0, 1):
            send_or_keep(
                weights[name].at[:, pl.ds(h * HALF, HALF)], S.at[n, a], quad[n] + 2 * h + a,
                device(z, x, yhi * 2 + b, h), jnp.logical_and(a == h, b == h),
            )

    gain_mate = take()
    send(gain, GM, gain_mate, mate)
    gain_in = pltpu.make_async_copy(gain, GO, rsem.at[take()])
    gain_in.start()

    def slot(yy, core):
        return E.at[yy % 2, (yy // 2) * 2 + core]

    def half(ref, i):
        return ref.at[pl.ds(i * 128, 128), :]

    e_p, e_m, e_op, e_om = take(2), take(2), take(), take()
    c_own, c_p, c_m, c_o = take(), take(2), take(2), take(2)
    for i in (0, 1):
        send(half(enc, i), half(slot(y, b), i), e_p + i, device(z, x, yp, b))
        send(half(enc, 1 - i), half(slot(y, b), 1 - i), e_m + 1 - i, device(z, x, ym, b))
    tok, tok_mate = take(), take()
    send(prev, T.at[a], tok, device(z, x, (yhi * 2 + b + 1) % NY, a))

    own = pltpu.make_async_copy(enc, slot(y, b), rsem.at[take()])
    own.start()
    send(enc, slot(y, b), c_own, mate)

    ax, az, bz, bx, bo = ([take(m) for _ in GROUPS] for m in (3, 8, 8, 16, 8))
    up, down = device(zp, x, y, b), device(zm, x, y, b)
    east, west = device(z, xp, y, b), device(z, xm, y, b)

    def zz(d):
        return (z + d + NZ) % NZ

    def pass_on(ref, i, to):
        send(ref, ref, i, to)

    def a_ring(g, step):
        ref, i = WA[g], az[g] + 2 * (step - 1)
        if step > 1:
            arrived(ref.at[zz(1 - step)], i - 2)
            arrived(ref.at[zz(step - 1)], i - 1)
        if step < 4:
            pass_on(ref.at[zz(1 - step)], i, up)
            pass_on(ref.at[zz(step - 1)], i + 1, down)
        else:
            pass_on(ref.at[zz(-3), pl.ds(0, 2)], i, up)
            pass_on(ref.at[zz(3), pl.ds(2, 2)], i + 1, down)

    def a_end(g):
        arrived(WA[g].at[zz(4), pl.ds(0, 2)], az[g] + 6)
        arrived(WA[g].at[zz(4), pl.ds(2, 2)], az[g] + 7)

    def b_ring(g, step):
        ref, i = WB[g].at[x], bz[g] + 2 * (step - 1)
        if step > 1:
            arrived(ref.at[zz(1 - step)], i - 2)
            arrived(ref.at[zz(step - 1)], i - 1)
        if step < 4:
            pass_on(ref.at[zz(1 - step)], i, up)
            pass_on(ref.at[zz(step - 1)], i + 1, down)
        else:
            pass_on(ref.at[zz(-3), :, pl.ds(0, 16), :], i, up)
            pass_on(ref.at[zz(3), :, pl.ds(16, 16), :], i + 1, down)

    def b_end(g):
        arrived(WB[g].at[x, zz(4), :, pl.ds(0, 16), :], bz[g] + 6)
        arrived(WB[g].at[x, zz(4), :, pl.ds(16, 16), :], bz[g] + 7)

    def b_out(g, *steps):
        for d in steps:
            block = WB[g].at[x, zz(d)]
            pass_on(block, bx[g] + 2 * (d % 8), east)
            pass_on(block, bx[g] + 2 * (d % 8) + 1, west)

    def b_on(g, *steps):
        for d in steps:
            arrived(WB[g].at[xm, zz(d)], bx[g] + 2 * (d % 8))
            arrived(WB[g].at[xp, zz(d)], bx[g] + 2 * (d % 8) + 1)
            if d <= 0:
                pass_on(WB[g].at[xm, zz(d)], bo[g] + d % 8, east)
            else:
                pass_on(WB[g].at[xp, zz(d)], bo[g] + d % 8, west)

    def b_far(g):
        for d in range(-3, 5):
            arrived(WB[g].at[xo, zz(d)], bo[g] + d % 8)

    def s1(g):
        used = sorted({w for units in GROUPS[g] for w, _ in units})
        for w in used:
            for i in (0, 1):
                arrived(S.at[names.index(w), i], quad[names.index(w)] + 2 * b + i)
        for path, units in enumerate(GROUPS[g]):
            for n, (w, u) in enumerate(units):
                unit = S[names.index(w), :, :, u * 128 : (u + 1) * 128].reshape(32, 128)
                if path == 0:
                    WA[g][z, x, n] = unit
                else:
                    WB[g][x, z, n] = unit
        b_ring(g, 1)
        for i, xi in enumerate((xp, xm, xo)):
            send(WA[g].at[z, x], WA[g].at[z, x], ax[g] + i, device(z, xi, y, b))
        b_out(g, 0)

    def s2(g):
        b_ring(g, 2)
        b_out(g, -1, 1)
        for i, xi in enumerate((xm, xp, xo)):
            arrived(WA[g].at[z, xi], ax[g] + i)
        a_ring(g, 1)

    def s3(g):
        b_ring(g, 3)
        b_out(g, -2, 2)
        b_on(g, 0)

    def s4(g):
        b_ring(g, 4)
        b_out(g, -3, 3)
        a_ring(g, 2)
        b_on(g, -1, 1)

    def s5(g):
        b_end(g)
        b_out(g, 4)
        b_on(g, -2, 2)

    def s6(g):
        a_ring(g, 3)
        b_on(g, -3, 3)

    def s7(g):
        a_ring(g, 4)
        b_on(g, 4)

    def s8(g):
        a_end(g)
        b_far(g)

    def e1():
        arrived(T.at[b], tok)
        send(T.at[b], T.at[b], tok_mate, mate)

    def e2():
        arrived(half(slot(ym, b), 0), e_p)
        send(half(slot(ym, b), 0), half(slot(ym, b), 0), e_op, device(z, x, yp, b))
        send(half(slot(ym, b), 0), half(slot(ym, b), 0), c_m, mate)
        arrived(half(slot(yp, b), 1), e_m + 1)
        send(half(slot(yp, b), 1), half(slot(yp, b), 1), e_om, device(z, x, ym, b))
        send(half(slot(yp, b), 1), half(slot(yp, b), 1), c_p + 1, mate)

    def e3():
        arrived(half(slot(ym, b), 1), e_p + 1)
        send(half(slot(ym, b), 1), half(slot(ym, b), 1), c_m + 1, mate)
        arrived(half(slot(yp, b), 0), e_m)
        send(half(slot(yp, b), 0), half(slot(yp, b), 0), c_p, mate)

    def e4():
        arrived(half(slot(yo, b), 0), e_op)
        send(half(slot(yo, b), 0), half(slot(yo, b), 0), c_o, mate)
        arrived(half(slot(yo, b), 1), e_om)
        send(half(slot(yo, b), 1), half(slot(yo, b), 1), c_o + 1, mate)

    def weight(w):
        units = []
        for u in range(4):
            for g, paths in enumerate(GROUPS):
                if (w, u) in paths[0]:
                    units.append(WA[g][:, :, paths[0].index((w, u))].reshape(D, 128))
                if (w, u) in paths[1]:
                    unit = WB[g][:, :, paths[1].index((w, u))]
                    units.append(jnp.swapaxes(unit, 0, 1).reshape(D, 128))
        return jnp.concatenate(units, axis=1)

    def cq():
        arrived(T.at[1 - b], tok_mate)
        arrived(GM, gain_mate)
        gain_in.wait()
        scale = jnp.where(a == b, GO[...], GM[...])
        normed = rms(T[...].reshape(2 * DEC, D).astype(F32), scale).astype(BF)
        Q[...] = dot(normed, weight("q")).astype(BF)

    def states(step):
        yy = (y + step) % NY
        return [
            (
                E[yy % 2, (yy // 2) * 2 + core],
                pl.ds(pl.multiple_of((yy % 2) * ENC + ((yy // 2) * 2 + core) * 256, 256), 256),
            )
            for core in (0, 1)
        ]

    def ready(step):
        if step == 0:
            own.wait()
            arrived(slot(y, 1 - b), c_own)
            return
        yy, sem = {1: (yp, c_p), 3: (ym, c_m), 2: (yo, c_o)}[step]
        for i in (0, 1):
            arrived(half(slot(yy, 1 - b), i), sem + i)

    def ck(step):
        ready(step)
        for block, rows in states(step):
            K[rows, :] = dot(block, weight("k")).astype(BF)

    def cv(step):
        for block, rows in states(step):
            V[rows, :] = dot(block, weight("v")).astype(BF)

    lane = lax.broadcasted_iota(jnp.int32, (DEC, 128), 1)

    def at(seq):
        @pl.loop(0, 4)
        def _(pair):
            columns = pl.ds(pl.multiple_of(pair * 128, 128), 128)
            rows = pl.ds(seq * DEC, DEC)
            keys = pl.ds(seq * ENC, ENC)
            q = Q[rows, columns]
            both = jnp.concatenate(
                [jnp.where(lane < 64, q, 0).astype(BF), jnp.where(lane >= 64, q, 0).astype(BF)],
                axis=0,
            )
            scores = lax.dot_general(
                both, K[keys, columns], (((1,), (1,)), ((), ())), preferred_element_type=F32
            )
            top = jnp.max(scores, axis=-1, keepdims=True)
            expo = jnp.exp((scores - top) * 0.125)
            probs = (expo * (1.0 / jnp.sum(expo, axis=-1, keepdims=True))).astype(BF)
            mixed2 = dot(probs, V[keys, columns])
            C[b, rows, columns] = jnp.where(lane < 64, mixed2[:DEC], mixed2[DEC:]).astype(BF)

    ctx, home = take(2), take(4)
    mine = pl.ds(pl.multiple_of(b * HALF, HALF), HALF)

    def cx(seq):
        own_half = C.at[b, pl.ds(seq * DEC, DEC), :]
        send(own_half, own_half, ctx + seq, mate)

    def op(seq):
        rows = pl.ds(seq * DEC, DEC)
        arrived(C.at[1 - b, rows, :], ctx + seq)
        wout = weight("o")
        attn = dot(C[0, rows, :], wout[:HALF]) + dot(C[1, rows, :], wout[HALF:])
        MX[seq] = (T[seq, :, mine].astype(F32) + attn).astype(BF)
        send_or_keep(
            MX.at[seq], H.at[b], home + 2 * seq + b, device(z, x, yhi * 2 + seq, a),
            jnp.logical_and(a == seq, b == seq),
        )

    def hm():
        for h in (0, 1):
            arrived(H.at[h], home + 2 * a + h)

    ops = dict(s1=s1, s2=s2, s3=s3, s4=s4, s5=s5, s6=s6, s7=s7, s8=s8, e1=e1, e2=e2, e3=e3, e4=e4,
               cq=cq, ck=ck, cv=cv, at=at, cx=cx, op=op, hm=hm, ld=load)
    for step in plan:
        name, _, arg = step.partition(" ")
        ops[name](*([int(arg)] if arg else []))

    return pending


CHUNKS = ((1, 5), (3, 7), (2, 6), (0, 4))


def experts_part(mixed, gain, routes_t, gates_t, loads, out,
                 G, U, DN, B0, BUF, X, XR, HID, OWN, PS, PX, RB, R, RR, PK, SP,
                 dsend, drecv, fsend, frecv, psend, precv, rsend, rrecv):
    z, x, y, b = place_of()
    sec, exp = lax.axis_index("section"), lax.axis_index("expert")
    here, a = exp // 2, exp % 2
    partner = (sec, exp + 1 - 2 * a)

    def zt(zk, sign):
        return (z + sign * zk + NZ) % NZ

    def xt(xk, sign):
        return (x + sign * xk + NX) % NX

    def plane(zi, xi):
        return (sec, (zi * NX + xi) * 2 + a)

    def remote(src, dst, s, r, to):
        return pltpu.make_async_remote_copy(
            src_ref=src, dst_ref=dst, send_sem=s, recv_sem=r, device_id=to, device_id_type=MESH
        )

    def to_blocks(rows):
        stacked = jnp.concatenate([rows[:, q * QUART : (q + 1) * QUART] for q in range(4)], axis=0)
        return dot(SP[...], stacked).astype(BF).reshape(4, 48, QUART)

    def to_rows(blocks, dst, first):
        stacked = dot(SP[...], blocks.reshape(192, QUART)).astype(BF)
        for q in range(4):
            dst[pl.ds(first, 48), q * QUART : (q + 1) * QUART] = stacked[q * 48 : (q + 1) * 48]

    moe_in = rms(mixed.astype(F32), gain[...]).astype(BF)
    expert_r = lax.broadcasted_iota(jnp.int32, (EXPERTS, DEC), 0)
    hot = [(expert_r == routes_t[k : k + 1, :]).astype(F32) for k in (0, 1)]
    t0 = lax.broadcasted_iota(jnp.int32, (DEC, DEC), 0)
    t1 = lax.broadcasted_iota(jnp.int32, (DEC, DEC), 1)
    count = dot((hot[0] + hot[1]).astype(BF), (t0 < t1).astype(BF))
    slot_id = lax.broadcasted_iota(jnp.int32, (SLOTS, DEC), 0)
    for k in (0, 1):
        slot = jnp.sum(count * hot[k], axis=0, keepdims=True).astype(jnp.int32)
        position = routes_t[k : k + 1, :] * CAP + slot
        PK[k] = (slot_id == position).astype(F32).astype(BF)
    place = PK[0] + PK[1]
    B0[...] = dot(place, moe_in).astype(BF)

    def rows_of(zi):
        return pl.ds(pl.multiple_of(zi * 48, 16), 48)

    def exchange(zi, first, zk, src, dst, s, r, sign):
        @pl.loop(first, NX)
        def _(xk):
            xi = xt(xk, sign)
            k = zk * NX + xk
            remote(src.at[zi * NX + xi], dst.at[here], s.at[k], r.at[k], plane(zi, xi)).start()

    for chunk in CHUNKS:
        for zk in chunk:
            zi = zt(zk, 1)
            BUF[pl.ds(zi * NX, NX)] = to_blocks(B0[rows_of(zi), :])
            exchange(zi, int(zk == 0), zk, BUF, X.at[0], dsend, drecv, 1)
    X[0, here] = BUF[here]

    def group(ref, zk):
        return ref.at[pl.ds(zt(zk, -1) * NX, NX)]

    def forward(chunk):
        for zk in chunk:
            zi = zt(zk, -1)

            @pl.loop(int(zk == 0), NX)
            def _(xk):
                src = X.at[0, zi * NX + xt(xk, -1)]
                remote(src, src, dsend.at[zk * NX + xk], drecv.at[zk * NX + xk], partner).wait_recv()

            remote(group(X.at[0], zk), group(X.at[1], zk), fsend.at[zk], frecv.at[zk], partner).start()

    def swap(j):
        return remote(PS.at[j], PX.at[j], psend.at[j], precv.at[j], partner)

    def work(j, chunk):
        for i, zk in enumerate(chunk):
            remote(group(X.at[1], zk), group(X.at[1], zk), fsend.at[zk], frecv.at[zk], partner).wait_recv()
            to_rows(group(X.at[0], zk)[...], XR, i * 48)
            to_rows(group(X.at[1], zk)[...], XR, 96 + i * 48)
        if j == 0:
            for load in loads:
                load.wait()
        rows = XR[...]
        gated, upper = dot(rows, G[...]), dot(rows, U[...])
        HID[...] = (jax.nn.gelu(gated) * upper).astype(BF)
        PS[j] = dot(HID[96:, :], DN[...]).astype(BF)
        swap(j).start()
        OWN[j] = dot(HID[:96, :], DN[...])

    def back(j, chunk):
        swap(j).wait()
        total = (OWN[j] + PX[j].astype(F32)).astype(BF)
        for i, zk in enumerate(chunk):
            zi = zt(zk, -1)
            RB[pl.ds(zi * NX, NX)] = to_blocks(total[i * 48 : (i + 1) * 48])
            exchange(zi, int(zk == 0), zk, RB, R, rsend, rrecv, -1)
            if zk == 0:
                R[here] = RB[here]

    for j in range(len(CHUNKS) + 2):
        if j < len(CHUNKS):
            forward(CHUNKS[j])
        if 1 <= j <= len(CHUNKS):
            work(j - 1, CHUNKS[j - 1])
        if j >= 2:
            back(j - 2, CHUNKS[j - 2])

    weights = [
        jnp.transpose(jnp.broadcast_to(gates_t[k : k + 1, :], (DEC, DEC)))[:, :1] for k in (0, 1)
    ]

    for chunk in CHUNKS:
        for zk in chunk:
            zi = zt(zk, 1)
            remote(group(X.at[0], zk), group(X.at[0], zk), fsend.at[zk], frecv.at[zk], partner).wait_send()

            @pl.loop(int(zk == 0), NX)
            def _(xk):
                k = zk * NX + xk
                block = R.at[zi * NX + xt(xk, 1)]
                remote(block, block, rsend.at[k], rrecv.at[k], partner).wait()
                remote(block, block, dsend.at[k], drecv.at[k], partner).wait_send()

            to_rows(R[pl.ds(zi * NX, NX)], RR, pl.multiple_of(zi * 48, 16))
    moe = [
        lax.dot_general(PK[k], RR[...], (((0,), (0,)), ((), ())), preferred_element_type=F32)
        * weights[k]
        for k in (0, 1)
    ]
    out[...] = (mixed.astype(F32) + (moe[0] + moe[1])).astype(BF)


def swap_matrix():
    row = lax.broadcasted_iota(jnp.int32, (192, 192), 0)
    column = lax.broadcasted_iota(jnp.int32, (192, 192), 1)
    part = lax.shift_right_logical(row * 171, 11)
    other = (part & 3) * 4 + lax.shift_right_logical(part, 2)
    return (column == other * CAP + (row - part * CAP)).astype(F32).astype(BF)


def relay_kernel(prev, enc, wq, wk, wv, wo, gain_attn, gain_moe, routes_t, gates_t,
                 wg, wu, wd, out, *scratch):
    first, second, wsem = scratch[:17], scratch[17:-1], scratch[-1]
    H = first[11]
    loads = [
        pltpu.make_async_copy(src, dst, wsem.at[i])
        for i, (src, dst) in enumerate(zip((wg, wu, wd), second[:3]))
    ]

    def load():
        second[15][...] = swap_matrix()
        for copy in loads:
            copy.start()

    pending = attention_part(
        PLAN, prev, enc, wq, wk, wv, wo, gain_attn, *first, load
    )
    mixed = jnp.concatenate([H[0], H[1]], axis=1)
    experts_part(mixed, gain_moe, routes_t, gates_t, loads, out, *second)
    for wait in pending:
        wait()


def relay(prev, enc, wq, wk, wv, wo, gain_attn, gain_moe, routes, gates, wg, wu, wd):
    vmem, hbm = pl.BlockSpec(memory_space=pltpu.VMEM), pl.BlockSpec(memory_space=pltpu.HBM)
    dma = pltpu.SemaphoreType.DMA
    return pl.pallas_call(
        relay_kernel,
        name="relay",
        out_shape=jax.ShapeDtypeStruct((DEC, D), BF),
        in_specs=[hbm] * 7 + [vmem] * 3 + [hbm] * 3,
        out_specs=vmem,
        scratch_shapes=[
            pltpu.VMEM((2, 4, 256, D), BF),
            pltpu.VMEM((NZ, NX, len(GROUPS[0][0]), 32, 128), BF),
            pltpu.VMEM((NX, NZ, len(GROUPS[0][1]), 32, 128), BF),
            pltpu.VMEM((NZ, NX, len(GROUPS[1][0]), 32, 128), BF),
            pltpu.VMEM((NX, NZ, len(GROUPS[1][1]), 32, 128), BF),
            pltpu.VMEM((2, DEC, D), BF),
            pltpu.VMEM((2 * ENC, HALF), BF),
            pltpu.VMEM((2 * ENC, HALF), BF),
            pltpu.VMEM((2 * DEC, HALF), BF),
            pltpu.VMEM((2, 2 * DEC, HALF), BF),
            pltpu.VMEM((2, DEC, HALF), BF),
            pltpu.VMEM((2, DEC, HALF), BF),
            pltpu.VMEM((1, D), F32),
            pltpu.VMEM((1, D), F32),
            pltpu.VMEM((4, 2, 16, HALF), BF),
            dma((SEMS_A,)),
            dma((SEMS_A,)),
            pltpu.VMEM((D, PIECE), BF),
            pltpu.VMEM((D, PIECE), BF),
            pltpu.VMEM((PIECE, D), BF),
            pltpu.VMEM((SLOTS, D), BF),
            pltpu.VMEM((32, 48, QUART), BF),
            pltpu.VMEM((2, 32, 48, QUART), BF),
            pltpu.VMEM((192, D), BF),
            pltpu.VMEM((192, PIECE), BF),
            pltpu.VMEM((4, 96, D), F32),
            pltpu.VMEM((4, 96, D), BF),
            pltpu.VMEM((4, 96, D), BF),
            pltpu.VMEM((32, 48, QUART), BF),
            pltpu.VMEM((32, 48, QUART), BF),
            pltpu.VMEM((SLOTS, D), BF),
            pltpu.VMEM((2, SLOTS, DEC), BF),
            pltpu.VMEM((192, 192), BF),
            dma((32,)),
            dma((32,)),
            dma((8,)),
            dma((8,)),
            dma((4,)),
            dma((4,)),
            dma((32,)),
            dma((32,)),
            dma((3,)),
        ],
        compiler_params=pltpu.CompilerParams(
            collective_id=1, has_side_effects=True, vmem_limit_bytes=60 << 20
        ),
    )(prev, enc, wq, wk, wv, wo, gain_attn, gain_moe, routes.T, gates.T, wg, wu, wd)


def per_device(previous, encoder_states, routes, gate_values, gain_attn, gain_moe, query_weight,
               key_weight, value_weight, out_weight, expert_gate, expert_up, expert_down):
    result = relay(
        previous[0, 0], encoder_states[0], query_weight[0], key_weight[0], value_weight[0],
        out_weight[0], gain_attn, gain_moe, routes[0, 0], gate_values[0, 0], expert_gate[0, 0],
        expert_up[0, 0], expert_down[0, 0],
    )
    return result.reshape(previous.shape)


def solution(mesh):
    in_specs = (
        P("section", "expert", None, None),
        P("expert", "section", None),
        P("section", "expert", None, None),
        P("section", "expert", None, None),
        P("section", None),
        P("section", None),
        P("section", "expert", None),
        P("section", "expert", None),
        P("section", "expert", None),
        P("section", "expert", None),
        P("section", "expert", None, None),
        P("section", "expert", None, None),
        P("section", "expert", None, None),
    )
    out_specs = P("section", "expert", None, None)
    return jax.shard_map(
        per_device, mesh=mesh, in_specs=in_specs, out_specs=out_specs, check_vma=False
    )
```

```python
import functools

import jax
import jax.numpy as jnp
from jax import lax
from jax.experimental import pallas as pl
from jax.experimental.pallas import tpu as pltpu
from jax.sharding import PartitionSpec as P

EXPERTS = 32
CAP = 12
NZ, NX, NY = 8, 4, 4
DEC, ENC, D = 128, 1024, 1024
HALF = D // 2
QUART = D // 4
PIECE = 1408
SLOTS = EXPERTS * CAP
EPS = 1e-06
MESH = pl.DeviceIdType.MESH
BF, F32 = jnp.bfloat16, jnp.float32


def place_of():
    s, e = lax.axis_index("section"), lax.axis_index("expert")
    return e // 8, (e // 2) % NX, (s // 2) * 2 + e % 2, s % 2


def device(z, x, y, core):
    return ((y // 2) * 2 + core, (z * NX + x) * 2 + y % 2)


class Sems:
    def __init__(self, ref):
        self.ref, self.used = ref, 0

    def take(self, count=1):
        first = self.used
        self.used += count
        return first


def rms(x, gain):
    return x * lax.rsqrt(jnp.mean(x * x, axis=-1, keepdims=True) + EPS) * gain


def dot(a, b):
    return jnp.dot(a, b, preferred_element_type=F32)


SEMS_A = 180


GROUPS = (
    (
        (("k", 0), ("k", 1), ("v", 0), ("v", 1), ("q", 0), ("q", 1)),
        (("k", 2), ("k", 3), ("v", 2), ("v", 3), ("q", 2), ("q", 3)),
    ),
    (
        (("o", 0),),
        (("o", 1), ("o", 2), ("o", 3)),
    ),
)


def make_plan(behind, places):
    plan = []
    for time in range(1, 9 + behind):
        plan += [f"s{time - g * behind} {g}" for g in (0, 1) if 1 <= time - g * behind <= 8]
        plan += places.get(time, [])
    return plan + places.get(0, [])


PLAN = make_plan(
    2,
    {
        5: ["e2"],
        7: ["e3", "e1"],
        8: ["e4", "ck 0", "ck 1"],
        6: ["ld"],
        9: ["ck 3", "ck 2", "cv 0", "cv 1", "cv 3", "cv 2", "cq", "at 0", "cx 0"],
        10: ["at 1", "cx 1", "op 0", "op 1", "hm"],
    },
)


def attention_part(plan, prev, enc, wq, wk, wv, wo, gain, E, WA0, WB0, WA1, WB1, T, K, V, Q, C, MX, H,
                   GM, GO, S, ssem, rsem, load):
    WA, WB = (WA0, WA1), (WB0, WB1)
    z, x, y, b = place_of()
    a, yhi = y % 2, y // 2
    zp, zm = (z + 1) % NZ, (z + NZ - 1) % NZ
    xp, xm, xo = (x + 1) % NX, (x + NX - 1) % NX, (x + 2) % NX
    yp, ym, yo = (y + 1) % NY, (y + NY - 1) % NY, (y + 2) % NY
    mate = device(z, x, y, 1 - b)
    take = Sems(rsem).take
    pending = []

    bar = pltpu.get_barrier_semaphore()
    shift_src = (y + 3) % NY
    greet = [
        mate,
        device(z, x, y + 1 - 2 * a, b),
        device(z, x, y + 1 - 2 * a, 1 - b),
        device(zp, x, y, b),
        device(zm, x, y, b),
        device(z, xp, y, b),
        device(z, xm, y, b),
        device(z, xo, y, b),
        device(z, x, yp, b),
        device(z, x, ym, b),
        device(z, x, (shift_src // 2) * 2 + b, shift_src % 2),
    ]
    for other in greet:
        pl.semaphore_signal(bar, inc=1, device_id=other, device_id_type=MESH)

    @pl.loop(1, 32)
    def _(k):
        zi, xi = (z + k // NX) % NZ, (x + k % NX) % NX
        pl.semaphore_signal(bar, inc=1, device_id=device(zi, xi, y, b), device_id_type=MESH)

    pl.semaphore_wait(bar, len(greet) + 31)

    def remote(src, dst, i, to):
        return pltpu.make_async_remote_copy(
            src_ref=src, dst_ref=dst, send_sem=ssem.at[i], recv_sem=rsem.at[i],
            device_id=to, device_id_type=MESH,
        )

    def send(src, dst, i, to):
        copy = remote(src, dst, i, to)
        copy.start()
        pending.append(copy.wait_send)

    def arrived(dst, i):
        remote(dst, dst, i, mate).wait_recv()

    def send_or_keep(src, dst, i, to, here):
        @pl.when(here)
        def _():
            pltpu.make_async_copy(src, dst, rsem.at[i]).start()

        @pl.when(jnp.logical_not(here))
        def _():
            remote(src, dst, i, to).start()

        def wait():
            @pl.when(jnp.logical_not(here))
            def _():
                remote(src, dst, i, to).wait_send()

        pending.append(wait)

    names = "kvqo"
    weights = dict(k=wk, v=wv, q=wq, o=wo)
    quad = [take(4) for _ in names]
    for n, name in enumerate(names):
        for h in (0, 1):
            send_or_keep(
                weights[name].at[:, pl.ds(h * HALF, HALF)], S.at[n, a], quad[n] + 2 * h + a,
                device(z, x, yhi * 2 + b, h), jnp.logical_and(a == h, b == h),
            )

    gain_mate = take()
    send(gain, GM, gain_mate, mate)
    gain_in = pltpu.make_async_copy(gain, GO, rsem.at[take()])
    gain_in.start()

    def slot(yy, core):
        return E.at[yy % 2, (yy // 2) * 2 + core]

    def half(ref, i):
        return ref.at[pl.ds(i * 128, 128), :]

    e_p, e_m, e_op, e_om = take(2), take(2), take(), take()
    c_own, c_p, c_m, c_o = take(), take(2), take(2), take(2)
    for i in (0, 1):
        send(half(enc, i), half(slot(y, b), i), e_p + i, device(z, x, yp, b))
        send(half(enc, 1 - i), half(slot(y, b), 1 - i), e_m + 1 - i, device(z, x, ym, b))
    tok, tok_mate = take(), take()
    send(prev, T.at[a], tok, device(z, x, (yhi * 2 + b + 1) % NY, a))

    own = pltpu.make_async_copy(enc, slot(y, b), rsem.at[take()])
    own.start()
    send(enc, slot(y, b), c_own, mate)

    ax, az, bz, bx, bo = ([take(m) for _ in GROUPS] for m in (3, 8, 8, 16, 8))
    up, down = device(zp, x, y, b), device(zm, x, y, b)
    east, west = device(z, xp, y, b), device(z, xm, y, b)

    def zz(d):
        return (z + d + NZ) % NZ

    def pass_on(ref, i, to):
        send(ref, ref, i, to)

    def a_ring(g, step):
        ref, i = WA[g], az[g] + 2 * (step - 1)
        if step > 1:
            arrived(ref.at[zz(1 - step)], i - 2)
            arrived(ref.at[zz(step - 1)], i - 1)
        if step < 4:
            pass_on(ref.at[zz(1 - step)], i, up)
            pass_on(ref.at[zz(step - 1)], i + 1, down)
        else:
            pass_on(ref.at[zz(-3), pl.ds(0, 2)], i, up)
            pass_on(ref.at[zz(3), pl.ds(2, 2)], i + 1, down)

    def a_end(g):
        arrived(WA[g].at[zz(4), pl.ds(0, 2)], az[g] + 6)
        arrived(WA[g].at[zz(4), pl.ds(2, 2)], az[g] + 7)

    def b_ring(g, step):
        ref, i = WB[g].at[x], bz[g] + 2 * (step - 1)
        if step > 1:
            arrived(ref.at[zz(1 - step)], i - 2)
            arrived(ref.at[zz(step - 1)], i - 1)
        if step < 4:
            pass_on(ref.at[zz(1 - step)], i, up)
            pass_on(ref.at[zz(step - 1)], i + 1, down)
        else:
            pass_on(ref.at[zz(-3), :, pl.ds(0, 16), :], i, up)
            pass_on(ref.at[zz(3), :, pl.ds(16, 16), :], i + 1, down)

    def b_end(g):
        arrived(WB[g].at[x, zz(4), :, pl.ds(0, 16), :], bz[g] + 6)
        arrived(WB[g].at[x, zz(4), :, pl.ds(16, 16), :], bz[g] + 7)

    def b_out(g, *steps):
        for d in steps:
            block = WB[g].at[x, zz(d)]
            pass_on(block, bx[g] + 2 * (d % 8), east)
            pass_on(block, bx[g] + 2 * (d % 8) + 1, west)

    def b_on(g, *steps):
        for d in steps:
            arrived(WB[g].at[xm, zz(d)], bx[g] + 2 * (d % 8))
            arrived(WB[g].at[xp, zz(d)], bx[g] + 2 * (d % 8) + 1)
            if d <= 0:
                pass_on(WB[g].at[xm, zz(d)], bo[g] + d % 8, east)
            else:
                pass_on(WB[g].at[xp, zz(d)], bo[g] + d % 8, west)

    def b_far(g):
        for d in range(-3, 5):
            arrived(WB[g].at[xo, zz(d)], bo[g] + d % 8)

    def s1(g):
        used = sorted({w for units in GROUPS[g] for w, _ in units})
        for w in used:
            for i in (0, 1):
                arrived(S.at[names.index(w), i], quad[names.index(w)] + 2 * b + i)
        for path, units in enumerate(GROUPS[g]):
            for n, (w, u) in enumerate(units):
                unit = S[names.index(w), :, :, u * 128 : (u + 1) * 128].reshape(32, 128)
                if path == 0:
                    WA[g][z, x, n] = unit
                else:
                    WB[g][x, z, n] = unit
        b_ring(g, 1)
        for i, xi in enumerate((xp, xm, xo)):
            send(WA[g].at[z, x], WA[g].at[z, x], ax[g] + i, device(z, xi, y, b))
        b_out(g, 0)

    def s2(g):
        b_ring(g, 2)
        b_out(g, -1, 1)
        for i, xi in enumerate((xm, xp, xo)):
            arrived(WA[g].at[z, xi], ax[g] + i)
        a_ring(g, 1)

    def s3(g):
        b_ring(g, 3)
        b_out(g, -2, 2)
        b_on(g, 0)

    def s4(g):
        b_ring(g, 4)
        b_out(g, -3, 3)
        a_ring(g, 2)
        b_on(g, -1, 1)

    def s5(g):
        b_end(g)
        b_out(g, 4)
        b_on(g, -2, 2)

    def s6(g):
        a_ring(g, 3)
        b_on(g, -3, 3)

    def s7(g):
        a_ring(g, 4)
        b_on(g, 4)

    def s8(g):
        a_end(g)
        b_far(g)

    def e1():
        arrived(T.at[b], tok)
        send(T.at[b], T.at[b], tok_mate, mate)

    def e2():
        arrived(half(slot(ym, b), 0), e_p)
        send(half(slot(ym, b), 0), half(slot(ym, b), 0), e_op, device(z, x, yp, b))
        send(half(slot(ym, b), 0), half(slot(ym, b), 0), c_m, mate)
        arrived(half(slot(yp, b), 1), e_m + 1)
        send(half(slot(yp, b), 1), half(slot(yp, b), 1), e_om, device(z, x, ym, b))
        send(half(slot(yp, b), 1), half(slot(yp, b), 1), c_p + 1, mate)

    def e3():
        arrived(half(slot(ym, b), 1), e_p + 1)
        send(half(slot(ym, b), 1), half(slot(ym, b), 1), c_m + 1, mate)
        arrived(half(slot(yp, b), 0), e_m)
        send(half(slot(yp, b), 0), half(slot(yp, b), 0), c_p, mate)

    def e4():
        arrived(half(slot(yo, b), 0), e_op)
        send(half(slot(yo, b), 0), half(slot(yo, b), 0), c_o, mate)
        arrived(half(slot(yo, b), 1), e_om)
        send(half(slot(yo, b), 1), half(slot(yo, b), 1), c_o + 1, mate)

    def weight(w):
        units = []
        for u in range(4):
            for g, paths in enumerate(GROUPS):
                if (w, u) in paths[0]:
                    units.append(WA[g][:, :, paths[0].index((w, u))].reshape(D, 128))
                if (w, u) in paths[1]:
                    unit = WB[g][:, :, paths[1].index((w, u))]
                    units.append(jnp.swapaxes(unit, 0, 1).reshape(D, 128))
        return jnp.concatenate(units, axis=1)

    def cq():
        arrived(T.at[1 - b], tok_mate)
        arrived(GM, gain_mate)
        gain_in.wait()
        scale = jnp.where(a == b, GO[...], GM[...])
        normed = rms(T[...].reshape(2 * DEC, D).astype(F32), scale).astype(BF)
        Q[...] = dot(normed, weight("q")).astype(BF)

    def states(step):
        yy = (y + step) % NY
        return [
            (
                E[yy % 2, (yy // 2) * 2 + core],
                pl.ds(pl.multiple_of((yy % 2) * ENC + ((yy // 2) * 2 + core) * 256, 256), 256),
            )
            for core in (0, 1)
        ]

    def ready(step):
        if step == 0:
            own.wait()
            arrived(slot(y, 1 - b), c_own)
            return
        yy, sem = {1: (yp, c_p), 3: (ym, c_m), 2: (yo, c_o)}[step]
        for i in (0, 1):
            arrived(half(slot(yy, 1 - b), i), sem + i)

    def ck(step):
        ready(step)
        for block, rows in states(step):
            K[rows, :] = dot(block, weight("k")).astype(BF)

    def cv(step):
        for block, rows in states(step):
            V[rows, :] = dot(block, weight("v")).astype(BF)

    lane = lax.broadcasted_iota(jnp.int32, (DEC, 128), 1)

    def at(seq):
        @pl.loop(0, 4, unroll=True)
        def _(pair):
            columns = pl.ds(pl.multiple_of(pair * 128, 128), 128)
            rows = pl.ds(seq * DEC, DEC)
            keys = pl.ds(seq * ENC, ENC)
            q = Q[rows, columns]
            both = jnp.concatenate(
                [jnp.where(lane < 64, q, 0).astype(BF), jnp.where(lane >= 64, q, 0).astype(BF)],
                axis=0,
            )
            scores = lax.dot_general(
                both, K[keys, columns], (((1,), (1,)), ((), ())), preferred_element_type=F32
            )
            top = jnp.max(scores, axis=-1, keepdims=True)
            expo = jnp.exp((scores - top) * 0.125)
            probs = (expo * (1.0 / jnp.sum(expo, axis=-1, keepdims=True))).astype(BF)
            mixed2 = dot(probs, V[keys, columns])
            C[b, rows, columns] = jnp.where(lane < 64, mixed2[:DEC], mixed2[DEC:]).astype(BF)

    ctx, home = take(2), take(4)
    mine = pl.ds(pl.multiple_of(b * HALF, HALF), HALF)

    def cx(seq):
        own_half = C.at[b, pl.ds(seq * DEC, DEC), :]
        send(own_half, own_half, ctx + seq, mate)

    def op(seq):
        rows = pl.ds(seq * DEC, DEC)
        arrived(C.at[1 - b, rows, :], ctx + seq)
        wout = weight("o")
        attn = dot(C[0, rows, :], wout[:HALF]) + dot(C[1, rows, :], wout[HALF:])
        MX[seq] = (T[seq, :, mine].astype(F32) + attn).astype(BF)
        send_or_keep(
            MX.at[seq], H.at[b], home + 2 * seq + b, device(z, x, yhi * 2 + seq, a),
            jnp.logical_and(a == seq, b == seq),
        )

    def hm():
        for h in (0, 1):
            arrived(H.at[h], home + 2 * a + h)

    ops = dict(s1=s1, s2=s2, s3=s3, s4=s4, s5=s5, s6=s6, s7=s7, s8=s8, e1=e1, e2=e2, e3=e3, e4=e4,
               cq=cq, ck=ck, cv=cv, at=at, cx=cx, op=op, hm=hm, ld=load)
    for step in plan:
        name, _, arg = step.partition(" ")
        ops[name](*([int(arg)] if arg else []))

    return pending


CHUNKS = ((1, 7), (2, 6), (3, 5), (4,), (0,))


def experts_part(mixed, gain, routes_t, gates_t, loads, out,
                 G, U, DN, B0, BUF, X, XR, HID, OWN, PS, PX, RB, R, RR, PK, SP,
                 dsend, drecv, fsend, frecv, psend, precv, rsend, rrecv):
    z, x, y, b = place_of()
    sec, exp = lax.axis_index("section"), lax.axis_index("expert")
    here, a = exp // 2, exp % 2
    partner = (sec, exp + 1 - 2 * a)

    def zt(zk, sign):
        return (z + sign * zk + NZ) % NZ

    def xt(xk, sign):
        return (x + sign * xk + NX) % NX

    def plane(zi, xi):
        return (sec, (zi * NX + xi) * 2 + a)

    def remote(src, dst, s, r, to):
        return pltpu.make_async_remote_copy(
            src_ref=src, dst_ref=dst, send_sem=s, recv_sem=r, device_id=to, device_id_type=MESH
        )

    def to_blocks(rows):
        stacked = jnp.concatenate([rows[:, q * QUART : (q + 1) * QUART] for q in range(4)], axis=0)
        return dot(SP[...], stacked).astype(BF).reshape(4, 48, QUART)

    def to_rows(blocks, dst, first):
        stacked = dot(SP[...], blocks.reshape(192, QUART)).astype(BF)
        for q in range(4):
            dst[pl.ds(first, 48), q * QUART : (q + 1) * QUART] = stacked[q * 48 : (q + 1) * 48]

    moe_in = rms(mixed.astype(F32), gain[...]).astype(BF)
    expert_r = lax.broadcasted_iota(jnp.int32, (EXPERTS, DEC), 0)
    hot = [(expert_r == routes_t[k : k + 1, :]).astype(F32) for k in (0, 1)]
    t0 = lax.broadcasted_iota(jnp.int32, (DEC, DEC), 0)
    t1 = lax.broadcasted_iota(jnp.int32, (DEC, DEC), 1)
    count = dot((hot[0] + hot[1]).astype(BF), (t0 < t1).astype(BF))
    slot_id = lax.broadcasted_iota(jnp.int32, (SLOTS, DEC), 0)
    for k in (0, 1):
        slot = jnp.sum(count * hot[k], axis=0, keepdims=True).astype(jnp.int32)
        position = routes_t[k : k + 1, :] * CAP + slot
        PK[k] = (slot_id == position).astype(F32).astype(BF)
    place = PK[0] + PK[1]
    B0[...] = dot(place, moe_in).astype(BF)

    def rows_of(zi):
        return pl.ds(pl.multiple_of(zi * 48, 16), 48)

    def exchange(zi, first, zk, src, dst, s, r, sign):
        @pl.loop(first, NX)
        def _(xk):
            xi = xt(xk, sign)
            k = zk * NX + xk
            remote(src.at[zi * NX + xi], dst.at[here], s.at[k], r.at[k], plane(zi, xi)).start()

    def dispatch(chunk):
        for zk in chunk:
            zi = zt(zk, 1)
            BUF[pl.ds(zi * NX, NX)] = to_blocks(B0[rows_of(zi), :])
            exchange(zi, int(zk == 0), zk, BUF, X.at[0], dsend, drecv, 1)
            if zk == 0:
                X[0, here] = BUF[here]

    for chunk in CHUNKS:
        dispatch(chunk)

    def group(ref, zk):
        return ref.at[pl.ds(zt(zk, -1) * NX, NX)]

    def forward(chunk):
        for zk in chunk:
            zi = zt(zk, -1)

            @pl.loop(int(zk == 0), NX)
            def _(xk):
                src = X.at[0, zi * NX + xt(xk, -1)]
                remote(src, src, dsend.at[zk * NX + xk], drecv.at[zk * NX + xk], partner).wait_recv()

            remote(group(X.at[0], zk), group(X.at[1], zk), fsend.at[zk], frecv.at[zk], partner).start()

    def part(j):
        return pl.ds(sum(len(chunk) for chunk in CHUNKS[:j]), len(CHUNKS[j]))

    def swap(j):
        return remote(PS.at[part(j)], PX.at[part(j)], psend.at[j], precv.at[j], partner)

    def work(j, chunk):
        half = 48 * len(chunk)
        for i, zk in enumerate(chunk):
            remote(group(X.at[1], zk), group(X.at[1], zk), fsend.at[zk], frecv.at[zk], partner).wait_recv()
            to_rows(group(X.at[0], zk)[...], XR, i * 48)
            to_rows(group(X.at[1], zk)[...], XR, half + i * 48)
        if j == 0:
            for load in loads:
                load.wait()
        rows = XR[: 2 * half, :]
        gated, upper = dot(rows, G[...]), dot(rows, U[...])
        HID[: 2 * half, :] = (jax.nn.gelu(gated) * upper).astype(BF)
        PS[part(j)] = dot(HID[half : 2 * half, :], DN[...]).astype(BF).reshape(len(chunk), 48, D)
        swap(j).start()
        OWN[part(j)] = dot(HID[:half, :], DN[...]).reshape(len(chunk), 48, D)

    def back(j, chunk):
        swap(j).wait()
        total = (OWN[part(j)] + PX[part(j)].astype(F32)).astype(BF)
        for i, zk in enumerate(chunk):
            zi = zt(zk, -1)
            RB[pl.ds(zi * NX, NX)] = to_blocks(total[i])
            exchange(zi, int(zk == 0), zk, RB, R, rsend, rrecv, -1)
            if zk == 0:
                R[here] = RB[here]

    for j in range(len(CHUNKS) + 2):
        if j < len(CHUNKS):
            forward(CHUNKS[j])
        if 1 <= j <= len(CHUNKS):
            work(j - 1, CHUNKS[j - 1])
        if j >= 2:
            back(j - 2, CHUNKS[j - 2])

    weights = [
        jnp.transpose(jnp.broadcast_to(gates_t[k : k + 1, :], (DEC, DEC)))[:, :1] for k in (0, 1)
    ]

    for chunk in CHUNKS:
        for zk in chunk:
            zi = zt(zk, 1)
            remote(group(X.at[0], zk), group(X.at[0], zk), fsend.at[zk], frecv.at[zk], partner).wait_send()

            @pl.loop(int(zk == 0), NX)
            def _(xk):
                k = zk * NX + xk
                block = R.at[zi * NX + xt(xk, 1)]
                remote(block, block, rsend.at[k], rrecv.at[k], partner).wait()
                remote(block, block, dsend.at[k], drecv.at[k], partner).wait_send()

            to_rows(R[pl.ds(zi * NX, NX)], RR, pl.multiple_of(zi * 48, 16))
    moe = [
        lax.dot_general(PK[k], RR[...], (((0,), (0,)), ((), ())), preferred_element_type=F32)
        * weights[k]
        for k in (0, 1)
    ]
    out[...] = (mixed.astype(F32) + (moe[0] + moe[1])).astype(BF)


def swap_matrix():
    row = lax.broadcasted_iota(jnp.int32, (192, 192), 0)
    column = lax.broadcasted_iota(jnp.int32, (192, 192), 1)
    part = lax.shift_right_logical(row * 171, 11)
    other = (part & 3) * 4 + lax.shift_right_logical(part, 2)
    return (column == other * CAP + (row - part * CAP)).astype(F32).astype(BF)


def relay_kernel(prev, enc, wq, wk, wv, wo, gain_attn, gain_moe, routes_t, gates_t,
                 wg, wu, wd, out, *scratch):
    first, second, wsem = scratch[:17], scratch[17:-1], scratch[-1]
    H = first[11]
    loads = [
        pltpu.make_async_copy(src, dst, wsem.at[i])
        for i, (src, dst) in enumerate(zip((wg, wu, wd), second[:3]))
    ]

    def load():
        second[15][...] = swap_matrix()
        for copy in loads:
            copy.start()

    pending = attention_part(
        PLAN, prev, enc, wq, wk, wv, wo, gain_attn, *first, load
    )
    mixed = jnp.concatenate([H[0], H[1]], axis=1)
    experts_part(mixed, gain_moe, routes_t, gates_t, loads, out, *second)
    for wait in pending:
        wait()


def relay(prev, enc, wq, wk, wv, wo, gain_attn, gain_moe, routes, gates, wg, wu, wd):
    vmem, hbm = pl.BlockSpec(memory_space=pltpu.VMEM), pl.BlockSpec(memory_space=pltpu.HBM)
    dma = pltpu.SemaphoreType.DMA
    return pl.pallas_call(
        relay_kernel,
        name="relay",
        out_shape=jax.ShapeDtypeStruct((DEC, D), BF),
        in_specs=[hbm] * 7 + [vmem] * 3 + [hbm] * 3,
        out_specs=vmem,
        scratch_shapes=[
            pltpu.VMEM((2, 4, 256, D), BF),
            pltpu.VMEM((NZ, NX, len(GROUPS[0][0]), 32, 128), BF),
            pltpu.VMEM((NX, NZ, len(GROUPS[0][1]), 32, 128), BF),
            pltpu.VMEM((NZ, NX, len(GROUPS[1][0]), 32, 128), BF),
            pltpu.VMEM((NX, NZ, len(GROUPS[1][1]), 32, 128), BF),
            pltpu.VMEM((2, DEC, D), BF),
            pltpu.VMEM((2 * ENC, HALF), BF),
            pltpu.VMEM((2 * ENC, HALF), BF),
            pltpu.VMEM((2 * DEC, HALF), BF),
            pltpu.VMEM((2, 2 * DEC, HALF), BF),
            pltpu.VMEM((2, DEC, HALF), BF),
            pltpu.VMEM((2, DEC, HALF), BF),
            pltpu.VMEM((1, D), F32),
            pltpu.VMEM((1, D), F32),
            pltpu.VMEM((4, 2, 16, HALF), BF),
            dma((SEMS_A,)),
            dma((SEMS_A,)),
            pltpu.VMEM((D, PIECE), BF),
            pltpu.VMEM((D, PIECE), BF),
            pltpu.VMEM((PIECE, D), BF),
            pltpu.VMEM((SLOTS, D), BF),
            pltpu.VMEM((32, 48, QUART), BF),
            pltpu.VMEM((2, 32, 48, QUART), BF),
            pltpu.VMEM((192, D), BF),
            pltpu.VMEM((192, PIECE), BF),
            pltpu.VMEM((8, 48, D), F32),
            pltpu.VMEM((8, 48, D), BF),
            pltpu.VMEM((8, 48, D), BF),
            pltpu.VMEM((32, 48, QUART), BF),
            pltpu.VMEM((32, 48, QUART), BF),
            pltpu.VMEM((SLOTS, D), BF),
            pltpu.VMEM((2, SLOTS, DEC), BF),
            pltpu.VMEM((192, 192), BF),
            dma((32,)),
            dma((32,)),
            dma((8,)),
            dma((8,)),
            dma((8,)),
            dma((8,)),
            dma((32,)),
            dma((32,)),
            dma((3,)),
        ],
        compiler_params=pltpu.CompilerParams(
            collective_id=1, has_side_effects=True, vmem_limit_bytes=60 << 20
        ),
    )(prev, enc, wq, wk, wv, wo, gain_attn, gain_moe, routes.T, gates.T, wg, wu, wd)


def per_device(previous, encoder_states, routes, gate_values, gain_attn, gain_moe, query_weight,
               key_weight, value_weight, out_weight, expert_gate, expert_up, expert_down):
    result = relay(
        previous[0, 0], encoder_states[0], query_weight[0], key_weight[0], value_weight[0],
        out_weight[0], gain_attn, gain_moe, routes[0, 0], gate_values[0, 0], expert_gate[0, 0],
        expert_up[0, 0], expert_down[0, 0],
    )
    return result.reshape(previous.shape)


def solution(mesh):
    in_specs = (
        P("section", "expert", None, None),
        P("expert", "section", None),
        P("section", "expert", None, None),
        P("section", "expert", None, None),
        P("section", None),
        P("section", None),
        P("section", "expert", None),
        P("section", "expert", None),
        P("section", "expert", None),
        P("section", "expert", None),
        P("section", "expert", None, None),
        P("section", "expert", None, None),
        P("section", "expert", None, None),
    )
    out_specs = P("section", "expert", None, None)
    return jax.shard_map(
        per_device, mesh=mesh, in_specs=in_specs, out_specs=out_specs, check_vma=False
    )
```

```python
import functools

import jax
import jax.numpy as jnp
from jax import lax
from jax.experimental import pallas as pl
from jax.experimental.pallas import tpu as pltpu
from jax.sharding import PartitionSpec as P

EXPERTS = 32
CAP = 12
NZ, NX, NY = 8, 4, 4
DEC, ENC, D = 128, 1024, 1024
HALF = D // 2
QUART = D // 4
PIECE = 1408
SLOTS = EXPERTS * CAP
EPS = 1e-06
MESH = pl.DeviceIdType.MESH
BF, F32 = jnp.bfloat16, jnp.float32


def place_of():
    s, e = lax.axis_index("section"), lax.axis_index("expert")
    return e // 8, (e // 2) % NX, (s // 2) * 2 + e % 2, s % 2


def device(z, x, y, core):
    return ((y // 2) * 2 + core, (z * NX + x) * 2 + y % 2)


class Sems:
    def __init__(self, ref):
        self.ref, self.used = ref, 0

    def take(self, count=1):
        first = self.used
        self.used += count
        return first


def rms(x, gain):
    return x * lax.rsqrt(jnp.mean(x * x, axis=-1, keepdims=True) + EPS) * gain


def dot(a, b):
    return jnp.dot(a, b, preferred_element_type=F32)


SEMS_A = 180


GROUPS = (
    (
        (("k", 0), ("k", 1), ("v", 0), ("v", 1), ("q", 0), ("q", 1)),
        (("k", 2), ("k", 3), ("v", 2), ("v", 3), ("q", 2), ("q", 3)),
    ),
    (
        (("o", 0),),
        (("o", 1), ("o", 2), ("o", 3)),
    ),
)


def make_plan(behind, places):
    plan = []
    for time in range(1, 9 + behind):
        plan += [f"s{time - g * behind} {g}" for g in (0, 1) if 1 <= time - g * behind <= 8]
        plan += places.get(time, [])
    return plan + places.get(0, [])


PLAN = make_plan(
    2,
    {
        5: ["e2"],
        7: ["e3", "e1"],
        8: ["e4", "ck 0", "ck 1"],
        6: ["ld"],
        9: ["ck 3", "ck 2", "cv 0", "cv 1", "cv 3", "cv 2", "cq", "at 0", "cx 0"],
        10: ["at 1", "cx 1", "op 0", "op 1", "hm"],
    },
)


def attention_part(plan, prev, enc, wq, wk, wv, wo, gain, E, WA0, WB0, WA1, WB1, T, K, V, Q, C, MX, H,
                   GM, GO, S, ssem, rsem, load):
    WA, WB = (WA0, WA1), (WB0, WB1)
    z, x, y, b = place_of()
    a, yhi = y % 2, y // 2
    zp, zm = (z + 1) % NZ, (z + NZ - 1) % NZ
    xp, xm, xo = (x + 1) % NX, (x + NX - 1) % NX, (x + 2) % NX
    yp, ym, yo = (y + 1) % NY, (y + NY - 1) % NY, (y + 2) % NY
    mate = device(z, x, y, 1 - b)
    take = Sems(rsem).take
    pending = []

    bar = pltpu.get_barrier_semaphore()
    shift_src = (y + 3) % NY
    greet = [
        mate,
        device(z, x, y + 1 - 2 * a, b),
        device(z, x, y + 1 - 2 * a, 1 - b),
        device(zp, x, y, b),
        device(zm, x, y, b),
        device(z, xp, y, b),
        device(z, xm, y, b),
        device(z, xo, y, b),
        device(z, x, yp, b),
        device(z, x, ym, b),
        device(z, x, (shift_src // 2) * 2 + b, shift_src % 2),
    ]
    for other in greet:
        pl.semaphore_signal(bar, inc=1, device_id=other, device_id_type=MESH)

    @pl.loop(1, 32)
    def _(k):
        zi, xi = (z + k // NX) % NZ, (x + k % NX) % NX
        pl.semaphore_signal(bar, inc=1, device_id=device(zi, xi, y, b), device_id_type=MESH)

    pl.semaphore_wait(bar, len(greet) + 31)

    def remote(src, dst, i, to):
        return pltpu.make_async_remote_copy(
            src_ref=src, dst_ref=dst, send_sem=ssem.at[i], recv_sem=rsem.at[i],
            device_id=to, device_id_type=MESH,
        )

    def send(src, dst, i, to):
        copy = remote(src, dst, i, to)
        copy.start()
        pending.append(copy.wait_send)

    def arrived(dst, i):
        remote(dst, dst, i, mate).wait_recv()

    def send_or_keep(src, dst, i, to, here):
        @pl.when(here)
        def _():
            pltpu.make_async_copy(src, dst, rsem.at[i]).start()

        @pl.when(jnp.logical_not(here))
        def _():
            remote(src, dst, i, to).start()

        def wait():
            @pl.when(jnp.logical_not(here))
            def _():
                remote(src, dst, i, to).wait_send()

        pending.append(wait)

    names = "kvqo"
    weights = dict(k=wk, v=wv, q=wq, o=wo)
    quad = [take(4) for _ in names]
    for n, name in enumerate(names):
        for h in (0, 1):
            send_or_keep(
                weights[name].at[:, pl.ds(h * HALF, HALF)], S.at[n, a], quad[n] + 2 * h + a,
                device(z, x, yhi * 2 + b, h), jnp.logical_and(a == h, b == h),
            )

    gain_mate = take()
    send(gain, GM, gain_mate, mate)
    gain_in = pltpu.make_async_copy(gain, GO, rsem.at[take()])
    gain_in.start()

    def slot(yy, core):
        return E.at[yy % 2, (yy // 2) * 2 + core]

    def half(ref, i):
        return ref.at[pl.ds(i * 128, 128), :]

    e_p, e_m, e_op, e_om = take(2), take(2), take(), take()
    c_own, c_p, c_m, c_o = take(), take(2), take(2), take(2)
    for i in (0, 1):
        send(half(enc, i), half(slot(y, b), i), e_p + i, device(z, x, yp, b))
        send(half(enc, 1 - i), half(slot(y, b), 1 - i), e_m + 1 - i, device(z, x, ym, b))
    tok, tok_mate = take(), take()
    send(prev, T.at[a], tok, device(z, x, (yhi * 2 + b + 1) % NY, a))

    own = pltpu.make_async_copy(enc, slot(y, b), rsem.at[take()])
    own.start()
    send(enc, slot(y, b), c_own, mate)

    ax, az, bz, bx, bo = ([take(m) for _ in GROUPS] for m in (3, 8, 8, 16, 8))
    up, down = device(zp, x, y, b), device(zm, x, y, b)
    east, west = device(z, xp, y, b), device(z, xm, y, b)

    def zz(d):
        return (z + d + NZ) % NZ

    def pass_on(ref, i, to):
        send(ref, ref, i, to)

    def a_ring(g, step):
        ref, i = WA[g], az[g] + 2 * (step - 1)
        if step > 1:
            arrived(ref.at[zz(1 - step)], i - 2)
            arrived(ref.at[zz(step - 1)], i - 1)
        if step < 4:
            pass_on(ref.at[zz(1 - step)], i, up)
            pass_on(ref.at[zz(step - 1)], i + 1, down)
        else:
            pass_on(ref.at[zz(-3), pl.ds(0, 2)], i, up)
            pass_on(ref.at[zz(3), pl.ds(2, 2)], i + 1, down)

    def a_end(g):
        arrived(WA[g].at[zz(4), pl.ds(0, 2)], az[g] + 6)
        arrived(WA[g].at[zz(4), pl.ds(2, 2)], az[g] + 7)

    def b_ring(g, step):
        ref, i = WB[g].at[x], bz[g] + 2 * (step - 1)
        if step > 1:
            arrived(ref.at[zz(1 - step)], i - 2)
            arrived(ref.at[zz(step - 1)], i - 1)
        if step < 4:
            pass_on(ref.at[zz(1 - step)], i, up)
            pass_on(ref.at[zz(step - 1)], i + 1, down)
        else:
            pass_on(ref.at[zz(-3), :, pl.ds(0, 16), :], i, up)
            pass_on(ref.at[zz(3), :, pl.ds(16, 16), :], i + 1, down)

    def b_end(g):
        arrived(WB[g].at[x, zz(4), :, pl.ds(0, 16), :], bz[g] + 6)
        arrived(WB[g].at[x, zz(4), :, pl.ds(16, 16), :], bz[g] + 7)

    def b_out(g, *steps):
        for d in steps:
            block = WB[g].at[x, zz(d)]
            pass_on(block, bx[g] + 2 * (d % 8), east)
            pass_on(block, bx[g] + 2 * (d % 8) + 1, west)

    def b_on(g, *steps):
        for d in steps:
            arrived(WB[g].at[xm, zz(d)], bx[g] + 2 * (d % 8))
            arrived(WB[g].at[xp, zz(d)], bx[g] + 2 * (d % 8) + 1)
            if d <= 0:
                pass_on(WB[g].at[xm, zz(d)], bo[g] + d % 8, east)
            else:
                pass_on(WB[g].at[xp, zz(d)], bo[g] + d % 8, west)

    def b_far(g):
        for d in range(-3, 5):
            arrived(WB[g].at[xo, zz(d)], bo[g] + d % 8)

    def s1(g):
        used = sorted({w for units in GROUPS[g] for w, _ in units})
        for w in used:
            for i in (0, 1):
                arrived(S.at[names.index(w), i], quad[names.index(w)] + 2 * b + i)
        for path, units in enumerate(GROUPS[g]):
            for n, (w, u) in enumerate(units):
                unit = S[names.index(w), :, :, u * 128 : (u + 1) * 128].reshape(32, 128)
                if path == 0:
                    WA[g][z, x, n] = unit
                else:
                    WB[g][x, z, n] = unit
        b_ring(g, 1)
        for i, xi in enumerate((xp, xm, xo)):
            send(WA[g].at[z, x], WA[g].at[z, x], ax[g] + i, device(z, xi, y, b))
        b_out(g, 0)

    def s2(g):
        b_ring(g, 2)
        b_out(g, -1, 1)
        for i, xi in enumerate((xm, xp, xo)):
            arrived(WA[g].at[z, xi], ax[g] + i)
        a_ring(g, 1)

    def s3(g):
        b_ring(g, 3)
        b_out(g, -2, 2)
        b_on(g, 0)

    def s4(g):
        b_ring(g, 4)
        b_out(g, -3, 3)
        a_ring(g, 2)
        b_on(g, -1, 1)

    def s5(g):
        b_end(g)
        b_out(g, 4)
        b_on(g, -2, 2)

    def s6(g):
        a_ring(g, 3)
        b_on(g, -3, 3)

    def s7(g):
        a_ring(g, 4)
        b_on(g, 4)

    def s8(g):
        a_end(g)
        b_far(g)

    def e1():
        arrived(T.at[b], tok)
        send(T.at[b], T.at[b], tok_mate, mate)

    def e2():
        arrived(half(slot(ym, b), 0), e_p)
        send(half(slot(ym, b), 0), half(slot(ym, b), 0), e_op, device(z, x, yp, b))
        send(half(slot(ym, b), 0), half(slot(ym, b), 0), c_m, mate)
        arrived(half(slot(yp, b), 1), e_m + 1)
        send(half(slot(yp, b), 1), half(slot(yp, b), 1), e_om, device(z, x, ym, b))
        send(half(slot(yp, b), 1), half(slot(yp, b), 1), c_p + 1, mate)

    def e3():
        arrived(half(slot(ym, b), 1), e_p + 1)
        send(half(slot(ym, b), 1), half(slot(ym, b), 1), c_m + 1, mate)
        arrived(half(slot(yp, b), 0), e_m)
        send(half(slot(yp, b), 0), half(slot(yp, b), 0), c_p, mate)

    def e4():
        arrived(half(slot(yo, b), 0), e_op)
        send(half(slot(yo, b), 0), half(slot(yo, b), 0), c_o, mate)
        arrived(half(slot(yo, b), 1), e_om)
        send(half(slot(yo, b), 1), half(slot(yo, b), 1), c_o + 1, mate)

    def weight(w):
        units = []
        for u in range(4):
            for g, paths in enumerate(GROUPS):
                if (w, u) in paths[0]:
                    units.append(WA[g][:, :, paths[0].index((w, u))].reshape(D, 128))
                if (w, u) in paths[1]:
                    unit = WB[g][:, :, paths[1].index((w, u))]
                    units.append(jnp.swapaxes(unit, 0, 1).reshape(D, 128))
        return jnp.concatenate(units, axis=1)

    def cq():
        arrived(T.at[1 - b], tok_mate)
        arrived(GM, gain_mate)
        gain_in.wait()
        scale = jnp.where(a == b, GO[...], GM[...])
        normed = rms(T[...].reshape(2 * DEC, D).astype(F32), scale).astype(BF)
        Q[...] = dot(normed, weight("q")).astype(BF)

    def states(step):
        yy = (y + step) % NY
        return [
            (
                E[yy % 2, (yy // 2) * 2 + core],
                pl.ds(pl.multiple_of((yy % 2) * ENC + ((yy // 2) * 2 + core) * 256, 256), 256),
            )
            for core in (0, 1)
        ]

    def ready(step):
        if step == 0:
            own.wait()
            arrived(slot(y, 1 - b), c_own)
            return
        yy, sem = {1: (yp, c_p), 3: (ym, c_m), 2: (yo, c_o)}[step]
        for i in (0, 1):
            arrived(half(slot(yy, 1 - b), i), sem + i)

    def ck(step):
        ready(step)
        for block, rows in states(step):
            K[rows, :] = dot(block, weight("k")).astype(BF)

    def cv(step):
        for block, rows in states(step):
            V[rows, :] = dot(block, weight("v")).astype(BF)

    lane = lax.broadcasted_iota(jnp.int32, (DEC, 128), 1)

    def at(seq):
        @pl.loop(0, 4, unroll=True)
        def _(pair):
            columns = pl.ds(pl.multiple_of(pair * 128, 128), 128)
            rows = pl.ds(seq * DEC, DEC)
            keys = pl.ds(seq * ENC, ENC)
            q = Q[rows, columns]
            both = jnp.concatenate(
                [jnp.where(lane < 64, q, 0).astype(BF), jnp.where(lane >= 64, q, 0).astype(BF)],
                axis=0,
            )
            scores = lax.dot_general(
                both, K[keys, columns], (((1,), (1,)), ((), ())), preferred_element_type=F32
            )
            top = jnp.max(scores, axis=-1, keepdims=True)
            expo = jnp.exp((scores - top) * 0.125)
            probs = (expo * (1.0 / jnp.sum(expo, axis=-1, keepdims=True))).astype(BF)
            mixed2 = dot(probs, V[keys, columns])
            C[b, rows, columns] = jnp.where(lane < 64, mixed2[:DEC], mixed2[DEC:]).astype(BF)

    ctx, home = take(2), take(4)
    mine = pl.ds(pl.multiple_of(b * HALF, HALF), HALF)

    def cx(seq):
        own_half = C.at[b, pl.ds(seq * DEC, DEC), :]
        send(own_half, own_half, ctx + seq, mate)

    def op(seq):
        rows = pl.ds(seq * DEC, DEC)
        arrived(C.at[1 - b, rows, :], ctx + seq)
        wout = weight("o")
        attn = dot(C[0, rows, :], wout[:HALF]) + dot(C[1, rows, :], wout[HALF:])
        MX[seq] = (T[seq, :, mine].astype(F32) + attn).astype(BF)
        send_or_keep(
            MX.at[seq], H.at[b], home + 2 * seq + b, device(z, x, yhi * 2 + seq, a),
            jnp.logical_and(a == seq, b == seq),
        )

    def hm():
        for h in (0, 1):
            arrived(H.at[h], home + 2 * a + h)

    ops = dict(s1=s1, s2=s2, s3=s3, s4=s4, s5=s5, s6=s6, s7=s7, s8=s8, e1=e1, e2=e2, e3=e3, e4=e4,
               cq=cq, ck=ck, cv=cv, at=at, cx=cx, op=op, hm=hm, ld=load)
    for step in plan:
        name, _, arg = step.partition(" ")
        ops[name](*([int(arg)] if arg else []))

    return pending


CHUNKS = ((1, 7), (2, 6), (3, 5), (4,), (0,))


def experts_part(mixed, gain, gates_t, loads, out,
                 G, U, DN, B0, BUF, X, XR, HID, OWN, PS, PX, RB, R, RR, PK, SP,
                 dsend, drecv, fsend, frecv, psend, precv, rsend, rrecv):
    z, x, y, b = place_of()
    sec, exp = lax.axis_index("section"), lax.axis_index("expert")
    here, a = exp // 2, exp % 2
    partner = (sec, exp + 1 - 2 * a)

    def zt(zk, sign):
        return (z + sign * zk + NZ) % NZ

    def xt(xk, sign):
        return (x + sign * xk + NX) % NX

    def plane(zi, xi):
        return (sec, (zi * NX + xi) * 2 + a)

    def remote(src, dst, s, r, to):
        return pltpu.make_async_remote_copy(
            src_ref=src, dst_ref=dst, send_sem=s, recv_sem=r, device_id=to, device_id_type=MESH
        )

    def to_blocks(rows):
        stacked = jnp.concatenate([rows[:, q * QUART : (q + 1) * QUART] for q in range(4)], axis=0)
        return dot(SP[...], stacked).astype(BF).reshape(4, 48, QUART)

    def to_rows(blocks, dst, first):
        stacked = dot(SP[...], blocks.reshape(192, QUART)).astype(BF)
        for q in range(4):
            dst[pl.ds(first, 48), q * QUART : (q + 1) * QUART] = stacked[q * 48 : (q + 1) * 48]

    moe_in = rms(mixed.astype(F32), gain[...]).astype(BF)
    place = PK[0] + PK[1]
    B0[...] = dot(place, moe_in).astype(BF)

    def rows_of(zi):
        return pl.ds(pl.multiple_of(zi * 48, 16), 48)

    def exchange(zi, first, zk, src, dst, s, r, sign):
        @pl.loop(first, NX)
        def _(xk):
            xi = xt(xk, sign)
            k = zk * NX + xk
            remote(src.at[zi * NX + xi], dst.at[here], s.at[k], r.at[k], plane(zi, xi)).start()

    def dispatch(chunk):
        for zk in chunk:
            zi = zt(zk, 1)
            BUF[pl.ds(zi * NX, NX)] = to_blocks(B0[rows_of(zi), :])
            exchange(zi, int(zk == 0), zk, BUF, X.at[0], dsend, drecv, 1)
            if zk == 0:
                X[0, here] = BUF[here]

    for chunk in CHUNKS:
        dispatch(chunk)

    def group(ref, zk):
        return ref.at[pl.ds(zt(zk, -1) * NX, NX)]

    def forward(chunk):
        for zk in chunk:
            zi = zt(zk, -1)

            @pl.loop(int(zk == 0), NX)
            def _(xk):
                src = X.at[0, zi * NX + xt(xk, -1)]
                remote(src, src, dsend.at[zk * NX + xk], drecv.at[zk * NX + xk], partner).wait_recv()

            remote(group(X.at[0], zk), group(X.at[1], zk), fsend.at[zk], frecv.at[zk], partner).start()

    def part(j):
        return pl.ds(sum(len(chunk) for chunk in CHUNKS[:j]), len(CHUNKS[j]))

    def swap(j):
        return remote(PS.at[part(j)], PX.at[part(j)], psend.at[j], precv.at[j], partner)

    def work(j, chunk):
        half = 48 * len(chunk)
        for i, zk in enumerate(chunk):
            remote(group(X.at[1], zk), group(X.at[1], zk), fsend.at[zk], frecv.at[zk], partner).wait_recv()
            to_rows(group(X.at[0], zk)[...], XR, i * 48)
            to_rows(group(X.at[1], zk)[...], XR, half + i * 48)
        if j == 0:
            for load in loads:
                load.wait()
        rows = XR[: 2 * half, :]
        gated, upper = dot(rows, G[...]), dot(rows, U[...])
        HID[: 2 * half, :] = (jax.nn.gelu(gated) * upper).astype(BF)
        PS[part(j)] = dot(HID[half : 2 * half, :], DN[...]).astype(BF).reshape(len(chunk), 48, D)
        swap(j).start()
        OWN[part(j)] = dot(HID[:half, :], DN[...]).reshape(len(chunk), 48, D)

    def back(j, chunk):
        swap(j).wait()
        total = (OWN[part(j)] + PX[part(j)].astype(F32)).astype(BF)
        for i, zk in enumerate(chunk):
            zi = zt(zk, -1)
            RB[pl.ds(zi * NX, NX)] = to_blocks(total[i])
            exchange(zi, int(zk == 0), zk, RB, R, rsend, rrecv, -1)
            if zk == 0:
                R[here] = RB[here]

    for j in range(len(CHUNKS) + 2):
        if j < len(CHUNKS):
            forward(CHUNKS[j])
        if 1 <= j <= len(CHUNKS):
            work(j - 1, CHUNKS[j - 1])
        if j >= 2:
            back(j - 2, CHUNKS[j - 2])

    weights = [
        jnp.transpose(jnp.broadcast_to(gates_t[k : k + 1, :], (DEC, DEC)))[:, :1] for k in (0, 1)
    ]

    for chunk in CHUNKS:
        for zk in chunk:
            zi = zt(zk, 1)
            remote(group(X.at[0], zk), group(X.at[0], zk), fsend.at[zk], frecv.at[zk], partner).wait_send()

            @pl.loop(int(zk == 0), NX)
            def _(xk):
                k = zk * NX + xk
                block = R.at[zi * NX + xt(xk, 1)]
                remote(block, block, rsend.at[k], rrecv.at[k], partner).wait()
                remote(block, block, dsend.at[k], drecv.at[k], partner).wait_send()

            to_rows(R[pl.ds(zi * NX, NX)], RR, pl.multiple_of(zi * 48, 16))
    moe = [
        lax.dot_general(PK[k], RR[...], (((0,), (0,)), ((), ())), preferred_element_type=F32)
        * weights[k]
        for k in (0, 1)
    ]
    out[...] = (mixed.astype(F32) + (moe[0] + moe[1])).astype(BF)


def slot_rows(routes_t, PK):
    expert_r = lax.broadcasted_iota(jnp.int32, (EXPERTS, DEC), 0)
    hot = [(expert_r == routes_t[k : k + 1, :]).astype(F32) for k in (0, 1)]
    t0 = lax.broadcasted_iota(jnp.int32, (DEC, DEC), 0)
    t1 = lax.broadcasted_iota(jnp.int32, (DEC, DEC), 1)
    count = dot((hot[0] + hot[1]).astype(BF), (t0 < t1).astype(BF))
    slot_id = lax.broadcasted_iota(jnp.int32, (SLOTS, DEC), 0)
    for k in (0, 1):
        slot = jnp.sum(count * hot[k], axis=0, keepdims=True).astype(jnp.int32)
        position = routes_t[k : k + 1, :] * CAP + slot
        PK[k] = (slot_id == position).astype(F32).astype(BF)


def swap_matrix():
    row = lax.broadcasted_iota(jnp.int32, (192, 192), 0)
    column = lax.broadcasted_iota(jnp.int32, (192, 192), 1)
    part = lax.shift_right_logical(row * 171, 11)
    other = (part & 3) * 4 + lax.shift_right_logical(part, 2)
    return (column == other * CAP + (row - part * CAP)).astype(F32).astype(BF)


def relay_kernel(prev, enc, wq, wk, wv, wo, gain_attn, gain_moe, routes_t, gates_t,
                 wg, wu, wd, out, *scratch):
    first, second, wsem = scratch[:17], scratch[17:-1], scratch[-1]
    H = first[11]
    loads = [
        pltpu.make_async_copy(src, dst, wsem.at[i])
        for i, (src, dst) in enumerate(zip((wg, wu, wd), second[:3]))
    ]

    def load():
        second[15][...] = swap_matrix()
        slot_rows(routes_t, second[14])
        for copy in loads:
            copy.start()

    pending = attention_part(
        PLAN, prev, enc, wq, wk, wv, wo, gain_attn, *first, load
    )
    mixed = jnp.concatenate([H[0], H[1]], axis=1)
    experts_part(mixed, gain_moe, gates_t, loads, out, *second)
    for wait in pending:
        wait()


def relay(prev, enc, wq, wk, wv, wo, gain_attn, gain_moe, routes, gates, wg, wu, wd):
    vmem, hbm = pl.BlockSpec(memory_space=pltpu.VMEM), pl.BlockSpec(memory_space=pltpu.HBM)
    dma = pltpu.SemaphoreType.DMA
    return pl.pallas_call(
        relay_kernel,
        name="relay",
        out_shape=jax.ShapeDtypeStruct((DEC, D), BF),
        in_specs=[hbm] * 7 + [vmem] * 3 + [hbm] * 3,
        out_specs=vmem,
        scratch_shapes=[
            pltpu.VMEM((2, 4, 256, D), BF),
            pltpu.VMEM((NZ, NX, len(GROUPS[0][0]), 32, 128), BF),
            pltpu.VMEM((NX, NZ, len(GROUPS[0][1]), 32, 128), BF),
            pltpu.VMEM((NZ, NX, len(GROUPS[1][0]), 32, 128), BF),
            pltpu.VMEM((NX, NZ, len(GROUPS[1][1]), 32, 128), BF),
            pltpu.VMEM((2, DEC, D), BF),
            pltpu.VMEM((2 * ENC, HALF), BF),
            pltpu.VMEM((2 * ENC, HALF), BF),
            pltpu.VMEM((2 * DEC, HALF), BF),
            pltpu.VMEM((2, 2 * DEC, HALF), BF),
            pltpu.VMEM((2, DEC, HALF), BF),
            pltpu.VMEM((2, DEC, HALF), BF),
            pltpu.VMEM((1, D), F32),
            pltpu.VMEM((1, D), F32),
            pltpu.VMEM((4, 2, 16, HALF), BF),
            dma((SEMS_A,)),
            dma((SEMS_A,)),
            pltpu.VMEM((D, PIECE), BF),
            pltpu.VMEM((D, PIECE), BF),
            pltpu.VMEM((PIECE, D), BF),
            pltpu.VMEM((SLOTS, D), BF),
            pltpu.VMEM((32, 48, QUART), BF),
            pltpu.VMEM((2, 32, 48, QUART), BF),
            pltpu.VMEM((192, D), BF),
            pltpu.VMEM((192, PIECE), BF),
            pltpu.VMEM((8, 48, D), F32),
            pltpu.VMEM((8, 48, D), BF),
            pltpu.VMEM((8, 48, D), BF),
            pltpu.VMEM((32, 48, QUART), BF),
            pltpu.VMEM((32, 48, QUART), BF),
            pltpu.VMEM((SLOTS, D), BF),
            pltpu.VMEM((2, SLOTS, DEC), BF),
            pltpu.VMEM((192, 192), BF),
            dma((32,)),
            dma((32,)),
            dma((8,)),
            dma((8,)),
            dma((8,)),
            dma((8,)),
            dma((32,)),
            dma((32,)),
            dma((3,)),
        ],
        compiler_params=pltpu.CompilerParams(
            collective_id=1, has_side_effects=True, vmem_limit_bytes=60 << 20
        ),
    )(prev, enc, wq, wk, wv, wo, gain_attn, gain_moe, routes.T, gates.T, wg, wu, wd)


def per_device(previous, encoder_states, routes, gate_values, gain_attn, gain_moe, query_weight,
               key_weight, value_weight, out_weight, expert_gate, expert_up, expert_down):
    result = relay(
        previous[0, 0], encoder_states[0], query_weight[0], key_weight[0], value_weight[0],
        out_weight[0], gain_attn, gain_moe, routes[0, 0], gate_values[0, 0], expert_gate[0, 0],
        expert_up[0, 0], expert_down[0, 0],
    )
    return result.reshape(previous.shape)


def solution(mesh):
    in_specs = (
        P("section", "expert", None, None),
        P("expert", "section", None),
        P("section", "expert", None, None),
        P("section", "expert", None, None),
        P("section", None),
        P("section", None),
        P("section", "expert", None),
        P("section", "expert", None),
        P("section", "expert", None),
        P("section", "expert", None),
        P("section", "expert", None, None),
        P("section", "expert", None, None),
        P("section", "expert", None, None),
    )
    out_specs = P("section", "expert", None, None)
    return jax.shard_map(
        per_device, mesh=mesh, in_specs=in_specs, out_specs=out_specs, check_vma=False
    )
```
